256 devices in a mesh: ulysses: 8 (over y, x_hi), blk: 32 (over x_lo, z, core).
Axes of the slice: x: 4 (x_hi: 2, x_lo: 2; x = x_hi * 2 + x_lo), y: 4, z: 8, core: 2. Of those that a mesh axis runs over, the one named last changes fastest.
Arguments:
- image_tokens: bfloat16 [8192, 3072], P(('blk', 'ulysses')), may hold values from -110 to 110
- text_tokens: bfloat16 [256, 3072], P('blk'), may hold values from -6 to 6
- modulation: float32 [3, 3072], replicated, may hold values from -4 to 4
- text_modulation: float32 [2, 3072], replicated, may hold values from -4 to 4
- norm_gains: float32 [3, 128], replicated, may hold values from 0.5 to 9
- qkv_weight: bfloat16 [3072, 24, 384], P(None, 'ulysses'), may hold values from -0.07289047 to 0.07289047
- text_kv_weight: bfloat16 [3072, 24, 256], P('blk', 'ulysses'), may hold values from -0.109375 to 0.109375
- out_weight: bfloat16 [3072, 3072], P('ulysses'), may hold values from -0.109375 to 0.109375
Outputs:
- block_out: bfloat16 [8192, 3072], P(('blk', 'ulysses'))
The draws below stay inside these ranges and needn't reach their ends.
All inputs are finite; a program needn't handle non-finite values.
Results may differ from the reference program's by a relative error of at most 0.015.
Values may be sent and summed in bfloat16 or wider, within the bound.
A program may use at most 128 MiB of HBM per device.

```python
import math
import jax
import jax.numpy as jnp
from jax import lax

D = 3072
HEADS = 24
HEAD = 128
TEXT = 256
TOKENS = 8192


def draw_image_tokens(key, part):
    key = jax.random.fold_in(key, 1)
    key_base = jax.random.fold_in(key, 0)
    values = jax.random.truncated_normal(key_base, -6.0, 6.0, (TOKENS, D), jnp.float32)
    return values.astype(jnp.bfloat16)


def draw_norm_gains(key, part):
    key = jax.random.fold_in(key, 2)
    key_drawn = jax.random.fold_in(key, 3)
    lower = jnp.array([[math.log(1.6)], [math.log(1.6)], [math.log(1.8)]], jnp.float32)
    upper = jnp.array([[math.log(2.6)], [math.log(2.6)], [math.log(3.0)]], jnp.float32)
    unit = jax.random.uniform(key_drawn, (3, HEAD), jnp.float32)
    gains = jnp.exp(lower + unit * (upper - lower))
    return gains.astype(jnp.float32)


def draw_qkv_weight(key, part):
    key = jax.random.fold_in(key, 3)
    key_entries = jax.random.fold_in(key, 0)
    entries = jax.random.truncated_normal(key_entries, -4.0, 4.0, (D, HEADS, 3 * HEAD), jnp.float32) / math.sqrt(D)
    return entries.astype(jnp.bfloat16)


def steps_of(key, dims, shards, smallest, top_value):
    def one(dim, parts):
        steps = jax.random.uniform(jax.random.fold_in(jax.random.fold_in(key, 6), dim), (parts,), jnp.float32, smallest / len(shards), top_value / len(shards))
        return jnp.repeat(jnp.exp(steps), dims[dim] // parts).reshape((-1,) + (1,) * (len(dims) - dim - 1))

    loudness = one(*shards[0])
    for cut in shards[1:]:
        loudness = loudness * one(*cut)
    return loudness


def gaussian(key, shape, scale, bound, pieces=(), dtype=jnp.bfloat16):
    values = scale * jax.random.normal(key, shape, jnp.float32)
    if pieces:
        values = values * steps_of(key, shape, pieces, -0.22, 0.18)
    return jnp.clip(values, -bound, bound).astype(dtype)


def setup_inputs(seed: int = 0) -> dict:
    key_list = jax.random.split(jax.random.key(seed), 9)
    image_tokens = draw_image_tokens(jax.random.fold_in(key_list[8], 71), 0)
    text_tokens = gaussian(key_list[1], (TEXT, D), 1.0, 6.0, ((0, 32),))
    modulation = gaussian(key_list[2], (3, D), 1.0, 4.0, (), jnp.float32)
    text_modulation = gaussian(key_list[3], (2, D), 1.0, 4.0, (), jnp.float32)
    norm_gains = draw_norm_gains(jax.random.fold_in(key_list[8], 71), 0)
    qkv_weight = draw_qkv_weight(jax.random.fold_in(key_list[8], 71), 0)
    text_kv_weight = gaussian(key_list[6], (D, HEADS, 2 * HEAD), D ** -0.5, 0.109375, ((0, 32), (1, 8)))
    out_weight = gaussian(key_list[7], (HEADS * HEAD, D), (HEADS * HEAD) ** -0.5, 0.109375, ((0, 8),))
    return {"image_tokens": image_tokens, "text_tokens": text_tokens, "modulation": modulation, "text_modulation": text_modulation, "norm_gains": norm_gains, "qkv_weight": qkv_weight, "text_kv_weight": text_kv_weight, "out_weight": out_weight}


def modulate(token_rows, shift, scale):
    values = token_rows.astype(jnp.float32)
    average = lax.optimization_barrier(jnp.mean(values, axis=-1, keepdims=True))
    spread = lax.optimization_barrier(jnp.mean((values - average) ** 2, axis=-1, keepdims=True))
    normed = (values - average) * lax.rsqrt(spread + 1e-06)
    return (normed * (1.0 + shift * 0.0 + scale) + shift).astype(jnp.bfloat16)

def root_normalize(values, gain):
    squares = lax.optimization_barrier(jnp.mean(values * values, axis=-1, keepdims=True))
    return (values * lax.rsqrt(squares + 1e-06) * gain).astype(jnp.bfloat16)

def one_head(inputs):
    query_head, key_head, value_head = inputs
    scores = jnp.dot(query_head, key_head.T, preferred_element_type=jnp.float32) * HEAD ** (-0.5)
    maximum = lax.optimization_barrier(jnp.max(scores, axis=-1, keepdims=True))
    expo = jnp.exp(scores - maximum)
    denominator = lax.optimization_barrier(jnp.sum(expo, axis=-1, keepdims=True))
    numerator = jnp.dot(expo.astype(jnp.bfloat16), value_head, preferred_element_type=jnp.float32)
    return (numerator / denominator).astype(jnp.bfloat16)

def reference(image_tokens, text_tokens, modulation, text_modulation, norm_gains, qkv_weight, text_kv_weight, out_weight):
    modulated = modulate(image_tokens, modulation[0], modulation[1])
    caption_mod = modulate(text_tokens, text_modulation[0], text_modulation[1])
    projected = jnp.dot(modulated, qkv_weight.reshape(D, HEADS * 3 * HEAD), preferred_element_type=jnp.float32)
    projected = projected.reshape(TOKENS, HEADS, 3, HEAD)
    queries = root_normalize(projected[:, :, 0], norm_gains[0])
    image_keys = root_normalize(projected[:, :, 1], norm_gains[1])
    image_values = projected[:, :, 2].astype(jnp.bfloat16)
    caption_projected = jnp.dot(caption_mod, text_kv_weight.reshape(D, HEADS * 2 * HEAD), preferred_element_type=jnp.float32)
    caption_projected = caption_projected.reshape(TEXT, HEADS, 2, HEAD)
    caption_keys = root_normalize(caption_projected[:, :, 0], norm_gains[2])
    caption_values = caption_projected[:, :, 1].astype(jnp.bfloat16)
    all_keys = jnp.concatenate([image_keys, caption_keys], axis=0)
    all_values = jnp.concatenate([image_values, caption_values], axis=0)
    attention = lax.map(one_head, (jnp.transpose(queries, (1, 0, 2)), jnp.transpose(all_keys, (1, 0, 2)), jnp.transpose(all_values, (1, 0, 2))))
    attention = jnp.transpose(attention, (1, 0, 2)).reshape(TOKENS, HEADS * HEAD)
    projection = jnp.dot(attention, out_weight, preferred_element_type=jnp.float32)
    return (image_tokens.astype(jnp.float32) + modulation[2] * projection).astype(jnp.bfloat16)
```

```python
import math

import jax
import jax.numpy as jnp
from jax import lax
from jax.experimental import pallas as pl
from jax.experimental.pallas import tpu as pltpu
from jax.sharding import PartitionSpec as P

D = 3072
HEAD = 128
HEADS_HERE = 3
ROWS = 32
BLOCK = 256
CAP_COLS = 96
CAP_ROWS = 8
CHUNKS = 4
CHUNK = D // CHUNKS
MESH = pl.DeviceIdType.MESH
F32 = jnp.float32
BF16 = jnp.bfloat16
QUERY_SCALE = math.log2(math.e) / math.sqrt(HEAD)
LOG2E = math.log2(math.e)
ULYSSES_STEPS = [(1, 0), (3, 0), (2, 0), (0, 1), (1, 1), (3, 1), (2, 1)]


def layer_norm(values, shift, scale):
    average = jnp.mean(values, axis=-1, keepdims=True)
    centered = values - average
    spread = jnp.mean(centered * centered, axis=-1, keepdims=True)
    return (centered * lax.rsqrt(spread + 1e-06) * (1.0 + scale) + shift).astype(BF16)


def root_norm(values, gain):
    squares = jnp.mean(values * values, axis=-1, keepdims=True)
    return (values * lax.rsqrt(squares + 1e-06) * gain).astype(BF16)


def kernel(
    img_ref, text_ref, mod_ref, tmod_ref, gains_ref, qkv_hbm, tkv_hbm, out_hbm,
    out_ref,
    w_qkv, w_cap, w_out, tok, cap_send, cap_recv, part, part_recv, cap_all,
    q_buf, kv, m_buf, acc, o_send, o_recv, l_send, l_recv, att, p_send, p_recv, p_own,
    w_sem, tok_send, tok_recv, cap_sems, part_sems, capall_sems,
    q_send, q_recv, right_send, right_recv, left_send, left_recv,
    o_ssem, o_rsem, l_ssem, l_rsem, p_ssem, p_rsem,
):
    u = lax.axis_index("ulysses")
    b = lax.axis_index("blk")
    y, xh = u // 2, lax.rem(u, 2)
    xl, z, c = b // 16, lax.rem(b // 2, 8), lax.rem(b, 2)

    def ulysses_peer(dy, dx):
        return lax.rem(y + dy, 4) * 2 + lax.rem(xh + dx, 2)

    def blk_of(xl_, z_, c_):
        return xl_ * 16 + z_ * 2 + c_

    load_cap = pltpu.make_async_copy(tkv_hbm, w_cap.at[:, pl.ds(0, CAP_COLS), :], w_sem.at[0])
    load_qkv = pltpu.make_async_copy(qkv_hbm, w_qkv, w_sem.at[1])
    load_out = pltpu.make_async_copy(out_hbm, w_out, w_sem.at[2])
    load_cap.start()
    load_qkv.start()
    load_out.start()

    barrier = pltpu.get_barrier_semaphore()
    for dy, dx in ULYSSES_STEPS:
        pl.semaphore_signal(
            barrier, inc=1, device_id={"ulysses": ulysses_peer(dy, dx)}, device_id_type=MESH
        )

    def greet(r, carry):
        pl.semaphore_signal(
            barrier, inc=1, device_id={"blk": lax.rem(b + r, 32)}, device_id_type=MESH
        )
        return carry

    lax.fori_loop(1, 32, greet, 0)

    tok[0] = layer_norm(img_ref[...].astype(F32), mod_ref[0:1, :], mod_ref[1:2, :])

    cap = layer_norm(text_ref[...].astype(F32), tmod_ref[0:1, :], tmod_ref[1:2, :]).astype(F32)
    groups = jnp.concatenate([cap[:, 384 * g : 384 * g + 384] for g in range(8)], axis=0)
    row = lax.broadcasted_iota(jnp.int32, (384, 512), 0)
    col = lax.broadcasted_iota(jnp.int32, (384, 512), 1)
    lane = lax.rem(col, 128)
    pick = jnp.where((lane < CAP_COLS) & (row == (col // 128) * CAP_COLS + lane), 1.0, 0.0)
    pieces = jnp.dot(groups.astype(BF16), pick.astype(BF16), preferred_element_type=F32)
    for g in range(8):
        for t in range(4):
            cap_send[4 * g + t] = pieces[8 * g : 8 * g + 8, 128 * t : 128 * t + 128]
    for h in range(HEADS_HERE):
        w_cap[h, CAP_COLS:128, :] = jnp.zeros((128 - CAP_COLS, 256), BF16)

    pl.semaphore_wait(barrier, 38)

    def send_caption(r, carry):
        to = lax.rem(b + r, 32)
        pltpu.make_async_remote_copy(
            src_ref=cap_send.at[to], dst_ref=cap_recv.at[b],
            send_sem=cap_sems.at[0], recv_sem=cap_sems.at[1],
            device_id={"blk": to}, device_id_type=MESH,
        ).start()
        return carry

    lax.fori_loop(1, 32, send_caption, 0)

    def token_copy(i):
        dy, dx = ULYSSES_STEPS[i]
        return pltpu.make_async_remote_copy(
            src_ref=tok.at[0], dst_ref=tok.at[i + 1],
            send_sem=tok_send.at[i], recv_sem=tok_recv.at[i],
            device_id={"ulysses": ulysses_peer(dy, dx)}, device_id_type=MESH,
        )

    for i in range(7):
        token_copy(i).start()

    cap_recv[b] = cap_send[b]
    load_cap.wait()
    cap_done = pltpu.make_async_remote_copy(
        src_ref=cap_send.at[pl.ds(0, 31)], dst_ref=cap_recv.at[pl.ds(0, 31)],
        send_sem=cap_sems.at[0], recv_sem=cap_sems.at[1],
        device_id={"blk": lax.rem(b + 1, 32)}, device_id_type=MESH,
    )
    cap_done.wait_recv()
    cap_rows = cap_recv[...].reshape(256, 128).astype(BF16)
    for h in range(HEADS_HERE):
        product = jnp.dot(cap_rows, w_cap[h], preferred_element_type=F32)
        both = jnp.concatenate(
            [product[:, :128].reshape(32, 8, 128), product[:, 128:].reshape(32, 8, 128)], axis=1
        )
        part[:, :, h * 128 : (h + 1) * 128] = both.astype(BF16)

    def send_part(r, carry):
        to = lax.rem(b + r, 32)
        pltpu.make_async_remote_copy(
            src_ref=part.at[to], dst_ref=part_recv.at[b],
            send_sem=part_sems.at[0], recv_sem=part_sems.at[1],
            device_id={"blk": to}, device_id_type=MESH,
        ).start()
        return carry

    lax.fori_loop(1, 32, send_part, 0)
    part_recv[b] = part[b]
    part_done = pltpu.make_async_remote_copy(
        src_ref=part.at[pl.ds(0, 31)], dst_ref=part_recv.at[pl.ds(0, 31)],
        send_sem=part_sems.at[0], recv_sem=part_sems.at[1],
        device_id={"blk": lax.rem(b + 1, 32)}, device_id_type=MESH,
    )
    part_done.wait_recv()
    total = jnp.sum(part_recv[...].astype(F32), axis=0)
    for h in range(HEADS_HERE):
        cols = slice(h * 128, (h + 1) * 128)
        key_rows = root_norm(total[0:8, cols], gains_ref[2:3, :]).astype(F32)
        cap_all[0, :, cols] = jnp.concatenate([key_rows, total[8:16, cols]], axis=0).astype(BF16)

    def capall_copy(dz):
        return pltpu.make_async_remote_copy(
            src_ref=cap_all.at[0], dst_ref=cap_all.at[dz],
            send_sem=capall_sems.at[0, dz], recv_sem=capall_sems.at[1, dz],
            device_id={"blk": blk_of(xl, lax.rem(z + dz, 8), c)}, device_id_type=MESH,
        )

    for dz in range(1, 8):
        capall_copy(dz).start()

    right_peer = {"blk": blk_of(xl, lax.rem(z + 1, 8), c)}
    left_peer = {"blk": blk_of(xl, lax.rem(z + 7, 8), c)}

    def ring_right(h, s):
        src, dst = kv.at[h, s - 1], kv.at[h, s]
        if s == 4:
            src, dst = src.at[0], dst.at[0]
        return pltpu.make_async_remote_copy(
            src_ref=src, dst_ref=dst, send_sem=right_send.at[h, s - 1],
            recv_sem=right_recv.at[h, s - 1], device_id=right_peer, device_id_type=MESH,
        )

    def ring_left(h, s):
        src, dst = kv.at[h, (9 - s) % 8], kv.at[h, 8 - s]
        if s == 4:
            src, dst = src.at[1], dst.at[1]
        return pltpu.make_async_remote_copy(
            src_ref=src, dst_ref=dst, send_sem=left_send.at[h, s - 1],
            recv_sem=left_recv.at[h, s - 1], device_id=left_peer, device_id_type=MESH,
        )

    def quad_peer(j):
        return {"blk": blk_of(lax.rem(xl + j // 2, 2), z, lax.rem(c + j % 2, 2))}

    def query_copy(h, j):
        return pltpu.make_async_remote_copy(
            src_ref=q_buf.at[h, 0], dst_ref=q_buf.at[h, j],
            send_sem=q_send.at[h, j], recv_sem=q_recv.at[h, j],
            device_id=quad_peer(j), device_id_type=MESH,
        )

    load_qkv.wait()
    for i in range(7):
        token_copy(i).wait_recv()

    def project(h, carry):
        rows = tok[...].reshape(BLOCK, D)
        projected = jnp.dot(rows, w_qkv[h], preferred_element_type=F32)
        kv[h, 0, 0] = root_norm(projected[:, 128:256], gains_ref[1:2, :])
        kv[h, 0, 1] = projected[:, 256:384].astype(BF16)
        ring_right(h, 1).start()
        ring_left(h, 1).start()
        q_buf[h, 0] = root_norm(projected[:, 0:128], gains_ref[0:1, :] * QUERY_SCALE)
        for j in range(1, 4):
            query_copy(h, j).start()
        return carry

    lax.fori_loop(0, HEADS_HERE, project, 0)

    ones = jnp.ones((BLOCK, 128), BF16)

    def attend(h, slots, first=False, caption=None):
        def tile(t, carry):
            q = q_buf[h, t]
            keys = [kv[h, s, 0] for s in slots]
            values = [kv[h, s, 1] for s in slots]
            fill = [ones for _ in slots]
            if caption is not None:
                keys.append(caption[0])
                values.append(caption[1])
                fill.append(jnp.ones((64, 128), BF16))
            scores = [
                lax.dot_general(q, k, (((1,), (1,)), ((), ())), preferred_element_type=F32)
                for k in keys
            ]
            top = jnp.max(scores[0], axis=-1, keepdims=True)
            for s in scores[1:]:
                top = jnp.maximum(top, jnp.max(s, axis=-1, keepdims=True))
            if first:
                m_new = jnp.broadcast_to(top, (BLOCK, 128))
            else:
                m_old = m_buf[h, t]
                m_new = jnp.maximum(m_old, top)
            wide = jnp.concatenate([m_new, m_new], axis=1)
            update = None
            for s, v, o in zip(scores, values, fill):
                sub = wide if s.shape[1] == 256 else m_new[:, : s.shape[1]]
                weights = jnp.exp2(s - sub).astype(BF16)
                term = jnp.dot(
                    weights, jnp.concatenate([v, o], axis=1), preferred_element_type=F32
                )
                update = term if update is None else update + term
            if first:
                acc[h, t] = update
            else:
                alpha = jnp.exp2(m_old - m_new)
                acc[h, t] = acc[h, t] * jnp.concatenate([alpha, alpha], axis=1) + update
            m_buf[h, t] = m_new
            return carry

        lax.fori_loop(0, 4, tile, 0)

    def forward(h, s):
        ring_right(h, s - 1).wait_recv()
        ring_right(h, s).start()
        ring_left(h, s - 1).wait_recv()
        ring_left(h, s).start()

    def step_two(h, carry):
        forward(h, 2)
        return carry

    lax.fori_loop(0, HEADS_HERE, step_two, 0)

    for dz in range(1, 8):
        capall_copy(dz).wait_recv()

    def step_three(h, carry):
        forward(h, 3)
        for j in range(1, 4):
            query_copy(h, j).wait_recv()
        col = pl.ds(pl.multiple_of(h * 128, 128), 128)
        cap_kv = cap_all[:, :, col].astype(F32)
        cap_keys = cap_kv[:, 0:8, :].reshape(64, 128).astype(BF16)
        cap_values = cap_kv[:, 8:16, :].reshape(64, 128).astype(BF16)
        attend(h, [0], first=True, caption=(cap_keys, cap_values))
        attend(h, [1, 7])
        return carry

    lax.fori_loop(0, HEADS_HERE, step_three, 0)

    def step_four(h, carry):
        forward(h, 4)
        attend(h, [2, 6])
        attend(h, [3, 5])
        return carry

    lax.fori_loop(0, HEADS_HERE, step_four, 0)

    def o_copy(h, j):
        return pltpu.make_async_remote_copy(
            src_ref=o_send.at[h, j], dst_ref=o_recv.at[h, j],
            send_sem=o_ssem.at[h, j], recv_sem=o_rsem.at[h, j],
            device_id=quad_peer(j), device_id_type=MESH,
        )

    def l_copy(h, j):
        return pltpu.make_async_remote_copy(
            src_ref=l_send.at[h, j], dst_ref=l_recv.at[h, j],
            send_sem=l_ssem.at[h, j], recv_sem=l_rsem.at[h, j],
            device_id=quad_peer(j), device_id_type=MESH,
        )

    def step_last(h, carry):
        ring_right(h, 4).wait_recv()
        ring_left(h, 4).wait_recv()
        attend(h, [4])
        for j in range(1, 4):
            denominator = acc[h, j, :, 128:]
            o_send[h, j] = (acc[h, j, :, :128] / denominator).astype(BF16)
            level = m_buf[h, j] + jnp.log(denominator) * LOG2E
            l_send[h, j] = level.T[0:8, :]
            o_copy(h, j).start()
            l_copy(h, j).start()
        return carry

    lax.fori_loop(0, HEADS_HERE, step_last, 0)

    def combine(h, carry):
        denominator = acc[h, 0, :, 128:]
        outs = [acc[h, 0, :, :128] / denominator]
        levels = [m_buf[h, 0] + jnp.log(denominator) * LOG2E]
        for j in range(1, 4):
            o_copy(h, j).wait_recv()
            l_copy(h, j).wait_recv()
            outs.append(o_recv[h, j].astype(F32))
            levels.append(jnp.broadcast_to(l_recv[h, j][0:1, :], (128, BLOCK)).T)
        top = levels[0]
        for level in levels[1:]:
            top = jnp.maximum(top, level)
        numerator, weight = None, None
        for out, level in zip(outs, levels):
            share = jnp.exp2(level - top)
            numerator = out * share if numerator is None else numerator + out * share
            weight = share if weight is None else weight + share
        att[h] = (numerator / weight).astype(BF16)
        return carry

    lax.fori_loop(0, HEADS_HERE, combine, 0)

    load_out.wait()

    def p_copy(n, i):
        dy, dx = ULYSSES_STEPS[i]
        return pltpu.make_async_remote_copy(
            src_ref=p_send.at[n, i], dst_ref=p_recv.at[n, i],
            send_sem=p_ssem.at[n, i], recv_sem=p_rsem.at[n, i],
            device_id={"ulysses": ulysses_peer(4 - dy, 2 - dx)}, device_id_type=MESH,
        )

    def out_chunk(n, carry):
        cols = pl.ds(pl.multiple_of(n * CHUNK, 128), CHUNK)
        rows = jnp.concatenate([att[h] for h in range(HEADS_HERE)], axis=1)
        product = jnp.dot(rows, w_out[:, cols], preferred_element_type=F32)
        p_own[n] = product[0:ROWS]
        p_send[n] = product[ROWS:].astype(BF16).reshape(7, ROWS, CHUNK)
        for i in range(7):
            p_copy(n, i).start()
        return carry

    lax.fori_loop(0, CHUNKS, out_chunk, 0)

    def finish(n, carry):
        cols = pl.ds(pl.multiple_of(n * CHUNK, 128), CHUNK)
        for i in range(7):
            p_copy(n, i).wait_recv()
        projection = p_own[n] + jnp.sum(p_recv[n].astype(F32), axis=0)
        out_ref[:, cols] = (
            img_ref[:, cols].astype(F32) + mod_ref[2:3, cols] * projection
        ).astype(BF16)
        return carry

    lax.fori_loop(0, CHUNKS, finish, 0)

    cap_done.wait_send()
    part_done.wait_send()
    for i in range(7):
        token_copy(i).wait_send()
    for dz in range(1, 8):
        capall_copy(dz).wait_send()

    def drain_head(h, carry):
        for s in range(1, 5):
            ring_right(h, s).wait_send()
            ring_left(h, s).wait_send()
        for j in range(1, 4):
            query_copy(h, j).wait_send()
            o_copy(h, j).wait_send()
            l_copy(h, j).wait_send()
        return carry

    lax.fori_loop(0, HEADS_HERE, drain_head, 0)

    def drain_chunk(n, carry):
        for i in range(7):
            p_copy(n, i).wait_send()
        return carry

    lax.fori_loop(0, CHUNKS, drain_chunk, 0)


def per_device(
    image_tokens, text_tokens, modulation, text_modulation, norm_gains,
    qkv_weight, text_kv_weight, out_weight,
):
    qkv = jnp.transpose(qkv_weight, (1, 0, 2))
    tkv = jnp.transpose(text_kv_weight, (1, 0, 2))
    dma = pltpu.SemaphoreType.DMA
    vmem = pl.BlockSpec(memory_space=pltpu.VMEM)
    hbm = pl.BlockSpec(memory_space=pl.ANY)
    h3 = HEADS_HERE
    return pl.pallas_call(
        kernel,
        out_shape=jax.ShapeDtypeStruct((ROWS, D), BF16),
        in_specs=[vmem] * 5 + [hbm] * 3,
        out_specs=vmem,
        scratch_shapes=[
            pltpu.VMEM((h3, D, 384), BF16),
            pltpu.VMEM((h3, 128, 256), BF16),
            pltpu.VMEM((384, D), BF16),
            pltpu.VMEM((8, ROWS, D), BF16),
            pltpu.VMEM((32, 8, 128), F32),
            pltpu.VMEM((32, 8, 128), F32),
            pltpu.VMEM((32, 16, 384), BF16),
            pltpu.VMEM((32, 16, 384), BF16),
            pltpu.VMEM((8, 16, 384), BF16),
            pltpu.VMEM((h3, 4, BLOCK, 128), BF16),
            pltpu.VMEM((h3, 8, 2, BLOCK, 128), BF16),
            pltpu.VMEM((h3, 4, BLOCK, 128), F32),
            pltpu.VMEM((h3, 4, BLOCK, 256), F32),
            pltpu.VMEM((h3, 4, BLOCK, 128), BF16),
            pltpu.VMEM((h3, 4, BLOCK, 128), BF16),
            pltpu.VMEM((h3, 4, 8, BLOCK), F32),
            pltpu.VMEM((h3, 4, 8, BLOCK), F32),
            pltpu.VMEM((h3, BLOCK, 128), BF16),
            pltpu.VMEM((CHUNKS, 7, ROWS, CHUNK), BF16),
            pltpu.VMEM((CHUNKS, 7, ROWS, CHUNK), BF16),
            pltpu.VMEM((CHUNKS, ROWS, CHUNK), F32),
            dma((3,)), dma((7,)), dma((7,)), dma((2,)), dma((2,)), dma((2, 8)),
            dma((h3, 4)), dma((h3, 4)),
            dma((h3, 4)), dma((h3, 4)), dma((h3, 4)), dma((h3, 4)),
            dma((h3, 4)), dma((h3, 4)), dma((h3, 4)), dma((h3, 4)),
            dma((CHUNKS, 7)), dma((CHUNKS, 7)),
        ],
        compiler_params=pltpu.CompilerParams(
            collective_id=0, has_side_effects=True, vmem_limit_bytes=50 * 1024 * 1024
        ),
        name="joint_attention",
    )(image_tokens, text_tokens, modulation, text_modulation, norm_gains, qkv, tkv, out_weight)


def solution(mesh):
    in_specs = (
        P(("blk", "ulysses"), None),
        P("blk", None),
        P(),
        P(),
        P(),
        P(None, "ulysses", None),
        P("blk", "ulysses", None),
        P("ulysses", None),
    )
    out_specs = P(("blk", "ulysses"), None)
    return jax.shard_map(
        per_device, mesh=mesh, in_specs=in_specs, out_specs=out_specs, check_vma=False
    )
```

```python
import math

import jax
import jax.numpy as jnp
from jax import lax
from jax.experimental import pallas as pl
from jax.experimental.pallas import tpu as pltpu
from jax.sharding import PartitionSpec as P

D = 3072
HEAD = 128
HEADS_HERE = 3
ROWS = 32
BLOCK = 256
PARTS = 2
PART = ROWS // PARTS
QUERIES = 1024
CAP_COLS = 96
CAP_ROWS = 8
CHUNKS = 4
CHUNK = D // CHUNKS
MESH = pl.DeviceIdType.MESH
F32 = jnp.float32
BF16 = jnp.bfloat16
QUERY_SCALE = math.log2(math.e) / math.sqrt(HEAD)
LOG2E = math.log2(math.e)
NEAR_STEPS = [(1, 0), (3, 0), (2, 0), (0, 1)]
TOKEN_HOPS = [
    (0, (1, 0)), (0, (3, 0)), (0, (2, 0)), (0, (0, 1)),
    (1, (0, 1)), (2, (0, 1)), (4, (2, 0)),
]
REDUCE_HOPS = [
    (5, (0, 1)), (6, (0, 1)), (7, (2, 0)), (3, (2, 0)),
    (1, (3, 0)), (2, (1, 0)), (4, (0, 1)),
]


def layer_norm(values, shift, scale):
    average = jnp.mean(values, axis=-1, keepdims=True)
    centered = values - average
    spread = jnp.mean(centered * centered, axis=-1, keepdims=True)
    return (centered * lax.rsqrt(spread + 1e-06) * (1.0 + scale) + shift).astype(BF16)


def root_norm(values, gain):
    squares = jnp.mean(values * values, axis=-1, keepdims=True)
    return (values * lax.rsqrt(squares + 1e-06) * gain).astype(BF16)


def kernel(
    img_hbm, text_hbm, mod_hbm, tmod_hbm, gains_hbm, qkv_hbm, tkv_hbm, out_hbm,
    out_ref,
    img_ref, text_ref, mod_ref, tmod_ref, gains_ref,
    w_qkv, w_cap, w_out, tok, a1_send, a1_recv, a2_send, a2_recv,
    part, r1_recv, r2_send, r2_recv, r3_send, r3_recv, cap_all,
    q_buf, kv, m_buf, acc, o_send, o_recv, l_send, l_recv, att, p_send, p_recv, p_keep,
    w_sem, tok_send, tok_recv, a_sems, r_sems, capall_sems,
    q_send, q_recv, right_send, right_recv, left_send, left_recv,
    o_ssem, o_rsem, l_ssem, l_rsem, p_ssem, p_rsem,
):
    u = lax.axis_index("ulysses")
    b = lax.axis_index("blk")
    y, xh = u // 2, lax.rem(u, 2)
    xl, z, c = b // 16, lax.rem(b // 2, 8), lax.rem(b, 2)

    def ulysses_peer(dy, dx):
        return lax.rem(y + dy, 4) * 2 + lax.rem(xh + dx, 2)

    def blk_of(xl_, z_, c_):
        return xl_ * 16 + z_ * 2 + c_

    def quad_peer(j):
        return {"blk": blk_of(lax.rem(xl + j // 2, 2), z, lax.rem(c + j % 2, 2))}

    def line_peer(dz):
        return {"blk": blk_of(xl, lax.rem(z + dz, 8), c)}

    load_cap = pltpu.make_async_copy(tkv_hbm, w_cap.at[:, pl.ds(0, CAP_COLS), :], w_sem.at[0])
    load_qkv = pltpu.make_async_copy(qkv_hbm, w_qkv, w_sem.at[1])
    load_out = pltpu.make_async_copy(out_hbm, w_out, w_sem.at[2])
    small = [
        pltpu.make_async_copy(src, dst, w_sem.at[3 + i])
        for i, (src, dst) in enumerate(
            [
                (img_hbm, img_ref),
                (mod_hbm, mod_ref),
                (text_hbm, text_ref),
                (tmod_hbm, tmod_ref),
                (gains_hbm, gains_ref),
            ]
        )
    ]
    for load in small:
        load.start()
    load_cap.start()
    load_qkv.start()
    load_out.start()

    barrier = pltpu.get_barrier_semaphore()
    for dy, dx in NEAR_STEPS:
        pl.semaphore_signal(
            barrier, inc=1, device_id={"ulysses": ulysses_peer(dy, dx)}, device_id_type=MESH
        )

    for j in range(1, 4):
        pl.semaphore_signal(barrier, inc=1, device_id=quad_peer(j), device_id_type=MESH)
    for dz in range(1, 8):
        pl.semaphore_signal(barrier, inc=1, device_id=line_peer(dz), device_id_type=MESH)

    small[0].wait()
    small[1].wait()
    normed = layer_norm(img_ref[...].astype(F32), mod_ref[0:1, :], mod_ref[1:2, :])
    for k in range(PARTS):
        tok[k, 0] = normed[k * PART : (k + 1) * PART]

    for load in small[2:]:
        load.wait()
    cap = layer_norm(text_ref[...].astype(F32), tmod_ref[0:1, :], tmod_ref[1:2, :]).astype(F32)
    groups = jnp.concatenate([cap[:, 384 * g : 384 * g + 384] for g in range(8)], axis=0)
    row = lax.broadcasted_iota(jnp.int32, (384, 512), 0)
    col = lax.broadcasted_iota(jnp.int32, (384, 512), 1)
    lane = lax.rem(col, 128)
    pick = jnp.where((lane < CAP_COLS) & (row == (col // 128) * CAP_COLS + lane), 1.0, 0.0)
    pieces = jnp.dot(groups.astype(BF16), pick.astype(BF16), preferred_element_type=F32)

    def piece(xl_, z_, c_):
        g, t = divmod(xl_ * 16 + z_ * 2 + c_, 4)
        return pieces[8 * g : 8 * g + 8, 128 * t : 128 * t + 128]

    for c_ in range(2):
        for xl_ in range(2):
            rows = jnp.concatenate([piece(xl_, z_, c_) for z_ in range(8)], axis=0)
            a1_send[c_ * 2 + xl_] = rows.astype(BF16)
    for h in range(HEADS_HERE):
        w_cap[h, CAP_COLS:128, :] = jnp.zeros((128 - CAP_COLS, 256), BF16)

    pl.semaphore_wait(barrier, 14)

    quad = c * 2 + xl

    def a1_copy(j):
        to = lax.rem(c + j % 2, 2) * 2 + lax.rem(xl + j // 2, 2)
        return pltpu.make_async_remote_copy(
            src_ref=a1_send.at[to], dst_ref=a1_recv.at[quad],
            send_sem=a_sems.at[0, j], recv_sem=a_sems.at[1, j],
            device_id=quad_peer(j), device_id_type=MESH,
        )

    def a2_copy(dz):
        return pltpu.make_async_remote_copy(
            src_ref=a2_send.at[lax.rem(z + dz, 8)], dst_ref=a2_recv.at[z],
            send_sem=a_sems.at[2, dz], recv_sem=a_sems.at[3, dz],
            device_id=line_peer(dz), device_id_type=MESH,
        )

    def token_copy(k, i):
        source, (dy, dx) = TOKEN_HOPS[i]
        return pltpu.make_async_remote_copy(
            src_ref=tok.at[k, source], dst_ref=tok.at[k, i + 1],
            send_sem=tok_send.at[k, i], recv_sem=tok_recv.at[k, i],
            device_id={"ulysses": ulysses_peer(dy, dx)}, device_id_type=MESH,
        )

    def token_near(k):
        for i in (3, 0, 1):
            token_copy(k, i).start()

    def token_onward(k):
        for source, onward in ((0, 4), (1, 5), (3, 6)):
            token_copy(k, source).wait_recv()
            token_copy(k, onward).start()
        token_copy(k, 2).start()

    def token_rest(k):
        for i in (2, 4, 5, 6):
            token_copy(k, i).wait_recv()

    for j in range(1, 4):
        a1_copy(j).start()
    token_near(0)

    a1_recv[quad] = a1_send[quad]
    for j in range(1, 4):
        a1_copy(j).wait_recv()
    by_quad = a1_recv[...].astype(F32)
    for z_ in range(8):
        rows = jnp.concatenate([by_quad[i, 8 * z_ : 8 * z_ + 8] for i in range(4)], axis=0)
        a2_send[z_] = rows.astype(BF16)
    for dz in range(1, 8):
        a2_copy(dz).start()
    a2_recv[z] = a2_send[z]

    token_onward(0)
    token_near(1)

    load_cap.wait()
    for dz in range(1, 8):
        a2_copy(dz).wait_recv()
    cap_rows = a2_recv[...].reshape(256, 128)
    for h in range(HEADS_HERE):
        product = jnp.dot(cap_rows, w_cap[h], preferred_element_type=F32)
        both = jnp.concatenate(
            [product[:, :128].reshape(8, 4, 8, 128), product[:, 128:].reshape(8, 4, 8, 128)],
            axis=2,
        )
        for i in range(4):
            part[i, :, :, h * 128 : (h + 1) * 128] = both[:, i].astype(BF16)

    other_c, other_xl = lax.rem(c + 1, 2), lax.rem(xl + 1, 2)
    r1_copy = pltpu.make_async_remote_copy(
        src_ref=part.at[pl.ds(other_c * 2, 2)], dst_ref=r1_recv,
        send_sem=r_sems.at[0, 0], recv_sem=r_sems.at[1, 0],
        device_id=quad_peer(1), device_id_type=MESH,
    )
    r1_copy.start()
    r2_copy = pltpu.make_async_remote_copy(
        src_ref=r2_send, dst_ref=r2_recv,
        send_sem=r_sems.at[0, 1], recv_sem=r_sems.at[1, 1],
        device_id=quad_peer(2), device_id_type=MESH,
    )

    def r3_copy(dz):
        return pltpu.make_async_remote_copy(
            src_ref=r3_send.at[lax.rem(z + dz, 8)], dst_ref=r3_recv.at[z],
            send_sem=r_sems.at[2, dz], recv_sem=r_sems.at[3, dz],
            device_id=line_peer(dz), device_id_type=MESH,
        )

    def capall_copy(dz):
        return pltpu.make_async_remote_copy(
            src_ref=cap_all.at[0], dst_ref=cap_all.at[dz],
            send_sem=capall_sems.at[0, dz], recv_sem=capall_sems.at[1, dz],
            device_id=line_peer(dz), device_id_type=MESH,
        )

    token_rest(0)
    token_onward(1)

    def ring_right(k, h, s):
        src, dst = kv.at[h, s - 1, k], kv.at[h, s, k]
        if s == 4:
            src, dst = src.at[0], dst.at[0]
        return pltpu.make_async_remote_copy(
            src_ref=src, dst_ref=dst, send_sem=right_send.at[k, h, s - 1],
            recv_sem=right_recv.at[k, h, s - 1], device_id=line_peer(1), device_id_type=MESH,
        )

    def ring_left(k, h, s):
        src, dst = kv.at[h, (9 - s) % 8, k], kv.at[h, 8 - s, k]
        if s == 4:
            src, dst = src.at[1], dst.at[1]
        return pltpu.make_async_remote_copy(
            src_ref=src, dst_ref=dst, send_sem=left_send.at[k, h, s - 1],
            recv_sem=left_recv.at[k, h, s - 1], device_id=line_peer(7), device_id_type=MESH,
        )

    def query_copy(h, j):
        return pltpu.make_async_remote_copy(
            src_ref=q_buf.at[h, 0], dst_ref=q_buf.at[h, j],
            send_sem=q_send.at[h, j], recv_sem=q_recv.at[h, j],
            device_id=quad_peer(j), device_id_type=MESH,
        )

    def project(k):
        def head(h, carry):
            rows = tok[k].reshape(PART * 8, D)
            projected = jnp.dot(rows, w_qkv[h], preferred_element_type=F32)
            kv[h, 0, k, 0] = root_norm(projected[:, 128:256], gains_ref[1:2, :])
            kv[h, 0, k, 1] = projected[:, 256:384].astype(BF16)
            ring_right(k, h, 1).start()
            ring_left(k, h, 1).start()
            q_buf[h, 0, k] = root_norm(projected[:, 0:128], gains_ref[0:1, :] * QUERY_SCALE)
            if k == PARTS - 1:
                for j in range(1, 4):
                    query_copy(h, j).start()
            return carry

        lax.fori_loop(0, HEADS_HERE, head, 0)

    load_qkv.wait()
    project(0)

    r1_copy.wait_recv()
    r2_send[...] = (part[c * 2 + other_xl].astype(F32) + r1_recv[other_xl].astype(F32)).astype(BF16)
    r2_copy.start()

    token_rest(1)
    project(1)

    r2_copy.wait_recv()
    r3_send[...] = (
        part[quad].astype(F32) + r1_recv[xl].astype(F32) + r2_recv[...].astype(F32)
    ).astype(BF16)
    for dz in range(1, 8):
        r3_copy(dz).start()
    r3_recv[z] = r3_send[z]

    def attend(h, slots, first=False, caption=None):
        q = q_buf[h].reshape(QUERIES, HEAD)
        keys = [jnp.concatenate([kv[h, s, k, 0] for k in range(PARTS)], axis=0) for s in slots]
        values = [jnp.concatenate([kv[h, s, k, 1] for k in range(PARTS)], axis=0) for s in slots]
        if caption is not None:
            keys.append(caption[0])
            values.append(caption[1])
        scores = [
            lax.dot_general(q, k, (((1,), (1,)), ((), ())), preferred_element_type=F32)
            for k in keys
        ]
        halves = [s[:, i : i + 128] for s in scores for i in range(0, s.shape[1], 128)]
        top = halves[0]
        for s in halves[1 : 2 * len(slots)]:
            top = jnp.maximum(top, s)
        top = jnp.max(top, axis=-1, keepdims=True)
        for s in halves[2 * len(slots) :]:
            top = jnp.maximum(top, jnp.max(s, axis=-1, keepdims=True))
        if first:
            m_new = jnp.broadcast_to(top, (QUERIES, 128))
        else:
            m_old = m_buf[h]
            m_new = jnp.maximum(m_old, top)
        wide = jnp.concatenate([m_new, m_new], axis=1)
        update = None
        for s, v in zip(scores, values):
            weights = jnp.exp2(s - wide[:, : s.shape[1]]).astype(BF16)
            filled = jnp.concatenate([v, jnp.ones(v.shape, BF16)], axis=1)
            term = jnp.dot(weights, filled, preferred_element_type=F32)
            update = term if update is None else update + term
        if first:
            acc[h] = update
        else:
            alpha = jnp.exp2(m_old - m_new)
            acc[h] = acc[h] * jnp.concatenate([alpha, alpha], axis=1) + update
        m_buf[h] = m_new

    def forward(k, h, s):
        ring_right(k, h, s - 1).wait_recv()
        ring_right(k, h, s).start()
        ring_left(k, h, s - 1).wait_recv()
        ring_left(k, h, s).start()

    def step_two(h, carry):
        forward(0, h, 2)
        return carry

    lax.fori_loop(0, HEADS_HERE, step_two, 0)

    for dz in range(1, 8):
        r3_copy(dz).wait_recv()
    total = jnp.sum(r3_recv[...].astype(F32), axis=0)
    for h in range(HEADS_HERE):
        cols = slice(h * 128, (h + 1) * 128)
        key_rows = root_norm(total[0:8, cols], gains_ref[2:3, :]).astype(F32)
        cap_all[0, :, cols] = jnp.concatenate([key_rows, total[8:16, cols]], axis=0).astype(BF16)
    for dz in range(1, 8):
        capall_copy(dz).start()

    def step_two_more(h, carry):
        forward(1, h, 2)
        return carry

    lax.fori_loop(0, HEADS_HERE, step_two_more, 0)

    def step_three_first(h, carry):
        forward(0, h, 3)
        return carry

    lax.fori_loop(0, HEADS_HERE, step_three_first, 0)

    def step_three(h, carry):
        forward(1, h, 3)
        for j in range(1, 4):
            query_copy(h, j).wait_recv()
        attend(h, [0, 1, 7], first=True)
        return carry

    lax.fori_loop(0, HEADS_HERE, step_three, 0)

    for dz in range(1, 8):
        capall_copy(dz).wait_recv()

    def step_four_first(h, carry):
        forward(0, h, 4)
        return carry

    lax.fori_loop(0, HEADS_HERE, step_four_first, 0)

    def step_four(h, carry):
        forward(1, h, 4)
        col = pl.ds(pl.multiple_of(h * 128, 128), 128)
        cap_kv = cap_all[:, :, col].astype(F32)
        cap_keys = cap_kv[:, 0:8, :].reshape(64, 128).astype(BF16)
        cap_values = cap_kv[:, 8:16, :].reshape(64, 128).astype(BF16)
        attend(h, [2, 6], caption=(cap_keys, cap_values))
        attend(h, [3, 5])
        return carry

    lax.fori_loop(0, HEADS_HERE, step_four, 0)

    def o_copy(h, j):
        return pltpu.make_async_remote_copy(
            src_ref=o_send.at[h, j], dst_ref=o_recv.at[h, j],
            send_sem=o_ssem.at[h, j], recv_sem=o_rsem.at[h, j],
            device_id=quad_peer(j), device_id_type=MESH,
        )

    def l_copy(h, j):
        return pltpu.make_async_remote_copy(
            src_ref=l_send.at[h, j], dst_ref=l_recv.at[h, j],
            send_sem=l_ssem.at[h, j], recv_sem=l_rsem.at[h, j],
            device_id=quad_peer(j), device_id_type=MESH,
        )

    def step_last(h, carry):
        for k in range(PARTS):
            ring_right(k, h, 4).wait_recv()
            ring_left(k, h, 4).wait_recv()
        attend(h, [4])
        for j in range(1, 4):
            rows = slice(j * BLOCK, (j + 1) * BLOCK)
            denominator = acc[h, rows, 128:]
            o_send[h, j] = (acc[h, rows, :128] / denominator).astype(BF16)
            level = m_buf[h, rows, :] + jnp.log(denominator) * LOG2E
            l_send[h, j] = level.T[0:8, :]
            o_copy(h, j).start()
            l_copy(h, j).start()
        return carry

    lax.fori_loop(0, HEADS_HERE, step_last, 0)

    def combine(h, carry):
        denominator = acc[h, 0:BLOCK, 128:]
        outs = [acc[h, 0:BLOCK, :128] / denominator]
        levels = [m_buf[h, 0:BLOCK, :] + jnp.log(denominator) * LOG2E]
        for j in range(1, 4):
            o_copy(h, j).wait_recv()
            l_copy(h, j).wait_recv()
            outs.append(o_recv[h, j].astype(F32))
            levels.append(jnp.broadcast_to(l_recv[h, j][0:1, :], (128, BLOCK)).T)
        top = levels[0]
        for level in levels[1:]:
            top = jnp.maximum(top, level)
        numerator, weight = None, None
        for out, level in zip(outs, levels):
            share = jnp.exp2(level - top)
            numerator = out * share if numerator is None else numerator + out * share
            weight = share if weight is None else weight + share
        att[h] = (numerator / weight).astype(BF16)
        return carry

    lax.fori_loop(0, HEADS_HERE, combine, 0)

    load_out.wait()

    def p_copy(n, i):
        source, (dy, dx) = REDUCE_HOPS[i]
        return pltpu.make_async_remote_copy(
            src_ref=p_send.at[n, source], dst_ref=p_recv.at[n, i],
            send_sem=p_ssem.at[n, i], recv_sem=p_rsem.at[n, i],
            device_id={"ulysses": ulysses_peer(dy, dx)}, device_id_type=MESH,
        )

    def out_chunk(n, carry):
        cols = pl.ds(pl.multiple_of(n * CHUNK, 128), CHUNK)
        rows = jnp.concatenate([att[h] for h in range(HEADS_HERE)], axis=1)
        product = jnp.dot(rows, w_out[:, cols], preferred_element_type=F32)
        product = product.reshape(PARTS, 8, PART, CHUNK)
        for i in (5, 6, 7, 3):
            p_send[n, i] = product[:, i].reshape(ROWS, CHUNK).astype(BF16)
        for i in range(4):
            p_copy(n, i).start()
        for k, i in enumerate((0, 1, 2, 4)):
            p_keep[n, k] = product[:, i].reshape(ROWS, CHUNK)
        return carry

    lax.fori_loop(0, CHUNKS, out_chunk, 0)

    def pass_on(n, carry):
        for k, i in ((1, 0), (2, 1), (3, 2)):
            p_copy(n, i).wait_recv()
            source = REDUCE_HOPS[i + 4][0]
            p_send[n, source] = (p_keep[n, k] + p_recv[n, i].astype(F32)).astype(BF16)
            p_copy(n, i + 4).start()
        return carry

    lax.fori_loop(0, CHUNKS, pass_on, 0)

    def finish(n, carry):
        cols = pl.ds(pl.multiple_of(n * CHUNK, 128), CHUNK)
        for i in range(3, 7):
            p_copy(n, i).wait_recv()
        projection = p_keep[n, 0] + jnp.sum(p_recv[n, 3:7].astype(F32), axis=0)
        out_ref[:, cols] = (
            img_ref[:, cols].astype(F32) + mod_ref[2:3, cols] * projection
        ).astype(BF16)
        return carry

    lax.fori_loop(0, CHUNKS, finish, 0)

    for j in range(1, 4):
        a1_copy(j).wait_send()
    r1_copy.wait_send()
    r2_copy.wait_send()
    for dz in range(1, 8):
        a2_copy(dz).wait_send()
        r3_copy(dz).wait_send()
        capall_copy(dz).wait_send()
    for k in range(PARTS):
        for i in range(7):
            token_copy(k, i).wait_send()

    def drain_head(h, carry):
        for s in range(1, 5):
            for k in range(PARTS):
                ring_right(k, h, s).wait_send()
                ring_left(k, h, s).wait_send()
        for j in range(1, 4):
            query_copy(h, j).wait_send()
            o_copy(h, j).wait_send()
            l_copy(h, j).wait_send()
        return carry

    lax.fori_loop(0, HEADS_HERE, drain_head, 0)

    def drain_chunk(n, carry):
        for i in range(7):
            p_copy(n, i).wait_send()
        return carry

    lax.fori_loop(0, CHUNKS, drain_chunk, 0)


def per_device(
    image_tokens, text_tokens, modulation, text_modulation, norm_gains,
    qkv_weight, text_kv_weight, out_weight,
):
    qkv = jnp.transpose(qkv_weight, (1, 0, 2))
    tkv = jnp.transpose(text_kv_weight, (1, 0, 2))
    dma = pltpu.SemaphoreType.DMA
    vmem = pl.BlockSpec(memory_space=pltpu.VMEM)
    hbm = pl.BlockSpec(memory_space=pl.ANY)
    h3 = HEADS_HERE
    return pl.pallas_call(
        kernel,
        out_shape=jax.ShapeDtypeStruct((ROWS, D), BF16),
        in_specs=[hbm] * 8,
        out_specs=vmem,
        scratch_shapes=[
            pltpu.VMEM((ROWS, D), BF16),
            pltpu.VMEM((CAP_ROWS, D), BF16),
            pltpu.VMEM((3, D), F32),
            pltpu.VMEM((2, D), F32),
            pltpu.VMEM((3, HEAD), F32),
            pltpu.VMEM((h3, D, 384), BF16),
            pltpu.VMEM((h3, 128, 256), BF16),
            pltpu.VMEM((384, D), BF16),
            pltpu.VMEM((PARTS, 8, PART, D), BF16),
            pltpu.VMEM((4, 64, 128), BF16),
            pltpu.VMEM((4, 64, 128), BF16),
            pltpu.VMEM((8, 32, 128), BF16),
            pltpu.VMEM((8, 32, 128), BF16),
            pltpu.VMEM((4, 8, 16, 384), BF16),
            pltpu.VMEM((2, 8, 16, 384), BF16),
            pltpu.VMEM((8, 16, 384), BF16),
            pltpu.VMEM((8, 16, 384), BF16),
            pltpu.VMEM((8, 16, 384), BF16),
            pltpu.VMEM((8, 16, 384), BF16),
            pltpu.VMEM((8, 16, 384), BF16),
            pltpu.VMEM((h3, 4, PARTS, BLOCK // PARTS, 128), BF16),
            pltpu.VMEM((h3, 8, PARTS, 2, BLOCK // PARTS, 128), BF16),
            pltpu.VMEM((h3, QUERIES, 128), F32),
            pltpu.VMEM((h3, QUERIES, 256), F32),
            pltpu.VMEM((h3, 4, BLOCK, 128), BF16),
            pltpu.VMEM((h3, 4, BLOCK, 128), BF16),
            pltpu.VMEM((h3, 4, 8, BLOCK), F32),
            pltpu.VMEM((h3, 4, 8, BLOCK), F32),
            pltpu.VMEM((h3, BLOCK, 128), BF16),
            pltpu.VMEM((CHUNKS, 8, ROWS, CHUNK), BF16),
            pltpu.VMEM((CHUNKS, 7, ROWS, CHUNK), BF16),
            pltpu.VMEM((CHUNKS, 4, ROWS, CHUNK), F32),
            dma((8,)), dma((PARTS, 7)), dma((PARTS, 7)), dma((4, 8)), dma((4, 8)), dma((2, 8)),
            dma((h3, 4)), dma((h3, 4)),
            dma((PARTS, h3, 4)), dma((PARTS, h3, 4)), dma((PARTS, h3, 4)), dma((PARTS, h3, 4)),
            dma((h3, 4)), dma((h3, 4)), dma((h3, 4)), dma((h3, 4)),
            dma((CHUNKS, 7)), dma((CHUNKS, 7)),
        ],
        compiler_params=pltpu.CompilerParams(
            collective_id=0, has_side_effects=True, vmem_limit_bytes=60 * 1024 * 1024
        ),
        name="joint_attention",
    )(image_tokens, text_tokens, modulation, text_modulation, norm_gains, qkv, tkv, out_weight)


def solution(mesh):
    in_specs = (
        P(("blk", "ulysses"), None),
        P("blk", None),
        P(),
        P(),
        P(),
        P(None, "ulysses", None),
        P("blk", "ulysses", None),
        P("ulysses", None),
    )
    out_specs = P(("blk", "ulysses"), None)
    return jax.shard_map(
        per_device, mesh=mesh, in_specs=in_specs, out_specs=out_specs, check_vma=False
    )
```

```python
import math

import jax
import jax.numpy as jnp
from jax import lax
from jax.experimental import pallas as pl
from jax.experimental.pallas import tpu as pltpu
from jax.sharding import PartitionSpec as P

D = 3072
HEAD = 128
HEADS_HERE = 3
ROWS = 32
BLOCK = 256
PARTS = 2
PART = ROWS // PARTS
QUERIES = 1024
CAP_COLS = 96
CAP_ROWS = 8
CHUNKS = 4
CHUNK = D // CHUNKS
MESH = pl.DeviceIdType.MESH
F32 = jnp.float32
BF16 = jnp.bfloat16
QUERY_SCALE = math.log2(math.e) / math.sqrt(HEAD)
LOG2E = math.log2(math.e)
NEAR_STEPS = [(1, 0), (3, 0), (2, 0), (0, 1)]
TOKEN_HOPS = [
    (0, (1, 0)), (0, (3, 0)), (0, (2, 0)), (0, (0, 1)),
    (1, (0, 1)), (2, (0, 1)), (4, (2, 0)),
]
REDUCE_HOPS = [
    (5, (0, 1)), (6, (0, 1)), (7, (2, 0)), (3, (2, 0)),
    (1, (3, 0)), (2, (1, 0)), (4, (0, 1)),
]


def layer_norm(values, shift, scale):
    average = jnp.mean(values, axis=-1, keepdims=True)
    centered = values - average
    spread = jnp.mean(centered * centered, axis=-1, keepdims=True)
    return (centered * lax.rsqrt(spread + 1e-06) * (1.0 + scale) + shift).astype(BF16)


def root_norm(values, gain):
    squares = jnp.mean(values * values, axis=-1, keepdims=True)
    return (values * lax.rsqrt(squares + 1e-06) * gain).astype(BF16)


def kernel(
    img_hbm, text_hbm, mod_hbm, tmod_hbm, gains_hbm, qkv_hbm, tkv_hbm, out_hbm,
    out_ref,
    img_ref, text_ref, mod_ref, tmod_ref, gains_ref,
    w_qkv, w_cap, w_out, tok, a1_send, a1_recv, a2_send, a2_recv,
    part, r1_recv, r2_send, r2_recv, r3_send, r3_recv, cap_all,
    q_buf, kv, m_buf, acc, o_send, o_recv, l_send, l_recv, ox_send, ox_recv, lx_send, lx_recv, att, p_send, p_recv, p_keep,
    w_sem, tok_send, tok_recv, a_sems, r_sems, capall_sems,
    q_send, q_recv, right_send, right_recv, left_send, left_recv,
    o_ssem, o_rsem, p_ssem, p_rsem,
):
    u = lax.axis_index("ulysses")
    b = lax.axis_index("blk")
    y, xh = u // 2, lax.rem(u, 2)
    xl, z, c = b // 16, lax.rem(b // 2, 8), lax.rem(b, 2)

    def ulysses_peer(dy, dx):
        return lax.rem(y + dy, 4) * 2 + lax.rem(xh + dx, 2)

    def blk_of(xl_, z_, c_):
        return xl_ * 16 + z_ * 2 + c_

    def quad_peer(j):
        return {"blk": blk_of(lax.rem(xl + j // 2, 2), z, lax.rem(c + j % 2, 2))}

    def line_peer(dz):
        return {"blk": blk_of(xl, lax.rem(z + dz, 8), c)}

    load_cap = pltpu.make_async_copy(tkv_hbm, w_cap.at[:, pl.ds(0, CAP_COLS), :], w_sem.at[0])
    load_qkv = pltpu.make_async_copy(qkv_hbm, w_qkv, w_sem.at[1])
    load_out = pltpu.make_async_copy(out_hbm, w_out, w_sem.at[2])
    small = [
        pltpu.make_async_copy(src, dst, w_sem.at[3 + i])
        for i, (src, dst) in enumerate(
            [
                (img_hbm, img_ref),
                (mod_hbm, mod_ref),
                (text_hbm, text_ref),
                (tmod_hbm, tmod_ref),
                (gains_hbm, gains_ref),
            ]
        )
    ]
    for load in small:
        load.start()
    load_cap.start()
    load_qkv.start()
    load_out.start()

    barrier = pltpu.get_barrier_semaphore()
    for dy, dx in NEAR_STEPS:
        pl.semaphore_signal(
            barrier, inc=1, device_id={"ulysses": ulysses_peer(dy, dx)}, device_id_type=MESH
        )

    for j in range(1, 4):
        pl.semaphore_signal(barrier, inc=1, device_id=quad_peer(j), device_id_type=MESH)
    for dz in range(1, 8):
        pl.semaphore_signal(barrier, inc=1, device_id=line_peer(dz), device_id_type=MESH)

    small[0].wait()
    small[1].wait()
    normed = layer_norm(img_ref[...].astype(F32), mod_ref[0:1, :], mod_ref[1:2, :])
    for k in range(PARTS):
        tok[k, 0] = normed[k * PART : (k + 1) * PART]

    for load in small[2:]:
        load.wait()
    cap = layer_norm(text_ref[...].astype(F32), tmod_ref[0:1, :], tmod_ref[1:2, :]).astype(F32)
    groups = jnp.concatenate([cap[:, 384 * g : 384 * g + 384] for g in range(8)], axis=0)
    row = lax.broadcasted_iota(jnp.int32, (384, 512), 0)
    col = lax.broadcasted_iota(jnp.int32, (384, 512), 1)
    lane = col & 127
    pick = jnp.where((lane < CAP_COLS) & (row == (col >> 7) * CAP_COLS + lane), 1.0, 0.0)
    pieces = jnp.dot(groups.astype(BF16), pick.astype(BF16), preferred_element_type=F32)

    def piece(xl_, z_, c_):
        g, t = divmod(xl_ * 16 + z_ * 2 + c_, 4)
        return pieces[8 * g : 8 * g + 8, 128 * t : 128 * t + 128]

    for c_ in range(2):
        for xl_ in range(2):
            rows = jnp.concatenate([piece(xl_, z_, c_) for z_ in range(8)], axis=0)
            a1_send[c_ * 2 + xl_] = rows.astype(BF16)
    for h in range(HEADS_HERE):
        w_cap[h, CAP_COLS:128, :] = jnp.zeros((128 - CAP_COLS, 256), BF16)

    pl.semaphore_wait(barrier, 14)

    quad = c * 2 + xl

    def a1_copy(j):
        to = lax.rem(c + j % 2, 2) * 2 + lax.rem(xl + j // 2, 2)
        return pltpu.make_async_remote_copy(
            src_ref=a1_send.at[to], dst_ref=a1_recv.at[quad],
            send_sem=a_sems.at[0, j], recv_sem=a_sems.at[1, j],
            device_id=quad_peer(j), device_id_type=MESH,
        )

    def a2_copy(dz):
        return pltpu.make_async_remote_copy(
            src_ref=a2_send.at[lax.rem(z + dz, 8)], dst_ref=a2_recv.at[z],
            send_sem=a_sems.at[2, dz], recv_sem=a_sems.at[3, dz],
            device_id=line_peer(dz), device_id_type=MESH,
        )

    def token_copy(k, i):
        source, (dy, dx) = TOKEN_HOPS[i]
        return pltpu.make_async_remote_copy(
            src_ref=tok.at[k, source], dst_ref=tok.at[k, i + 1],
            send_sem=tok_send.at[k, i], recv_sem=tok_recv.at[k, i],
            device_id={"ulysses": ulysses_peer(dy, dx)}, device_id_type=MESH,
        )

    def token_near(k):
        for i in (3, 0, 1):
            token_copy(k, i).start()

    def token_onward(k):
        for source, onward in ((0, 4), (1, 5), (3, 6)):
            token_copy(k, source).wait_recv()
            token_copy(k, onward).start()
        token_copy(k, 2).start()

    def token_rest(k):
        for i in (2, 4, 5, 6):
            token_copy(k, i).wait_recv()

    for j in range(1, 4):
        a1_copy(j).start()
    token_near(0)

    other_c, other_xl = lax.rem(c + 1, 2), lax.rem(xl + 1, 2)
    r1_copy = pltpu.make_async_remote_copy(
        src_ref=part.at[pl.ds(other_c * 2, 2)], dst_ref=r1_recv,
        send_sem=r_sems.at[0, 0], recv_sem=r_sems.at[1, 0],
        device_id=quad_peer(1), device_id_type=MESH,
    )
    r2_copy = pltpu.make_async_remote_copy(
        src_ref=r2_send, dst_ref=r2_recv,
        send_sem=r_sems.at[0, 1], recv_sem=r_sems.at[1, 1],
        device_id=quad_peer(2), device_id_type=MESH,
    )

    def r3_copy(dz):
        return pltpu.make_async_remote_copy(
            src_ref=r3_send.at[lax.rem(z + dz, 8)], dst_ref=r3_recv.at[z],
            send_sem=r_sems.at[2, dz], recv_sem=r_sems.at[3, dz],
            device_id=line_peer(dz), device_id_type=MESH,
        )

    def capall_copy(dz):
        return pltpu.make_async_remote_copy(
            src_ref=cap_all.at[0], dst_ref=cap_all.at[dz],
            send_sem=capall_sems.at[0, dz], recv_sem=capall_sems.at[1, dz],
            device_id=line_peer(dz), device_id_type=MESH,
        )

    def ring_right(k, h, s):
        src, dst = kv.at[h, s - 1, k], kv.at[h, s, k]
        if s == 4:
            src, dst = src.at[0], dst.at[0]
        return pltpu.make_async_remote_copy(
            src_ref=src, dst_ref=dst, send_sem=right_send.at[k, h, s - 1],
            recv_sem=right_recv.at[k, h, s - 1], device_id=line_peer(1), device_id_type=MESH,
        )

    def ring_left(k, h, s):
        src, dst = kv.at[h, (9 - s) % 8, k], kv.at[h, 8 - s, k]
        if s == 4:
            src, dst = src.at[1], dst.at[1]
        return pltpu.make_async_remote_copy(
            src_ref=src, dst_ref=dst, send_sem=left_send.at[k, h, s - 1],
            recv_sem=left_recv.at[k, h, s - 1], device_id=line_peer(7), device_id_type=MESH,
        )

    def query_copy(h, j):
        return pltpu.make_async_remote_copy(
            src_ref=q_buf.at[h, 0], dst_ref=q_buf.at[h, j],
            send_sem=q_send.at[h, j], recv_sem=q_recv.at[h, j],
            device_id=quad_peer(j), device_id_type=MESH,
        )

    def forward(k, h, s):
        ring_right(k, h, s - 1).wait_recv()
        ring_right(k, h, s).start()
        ring_left(k, h, s - 1).wait_recv()
        ring_left(k, h, s).start()

    def project(k):
        def head(h, carry):
            rows = tok[k].reshape(PART * 8, D)
            projected = jnp.dot(rows, w_qkv[h], preferred_element_type=F32)
            kv[h, 0, k, 0] = root_norm(projected[:, 128:256], gains_ref[1:2, :])
            kv[h, 0, k, 1] = projected[:, 256:384].astype(BF16)
            ring_right(k, h, 1).start()
            ring_left(k, h, 1).start()
            q_buf[h, 0, k] = root_norm(projected[:, 0:128], gains_ref[0:1, :] * QUERY_SCALE)
            if k == PARTS - 1:
                for j in range(1, 4):
                    query_copy(h, j).start()
            return carry

        lax.fori_loop(0, HEADS_HERE, head, 0)

    def cap_columns():
        a1_recv[quad] = a1_send[quad]
        for j in range(1, 4):
            a1_copy(j).wait_recv()
        by_quad = a1_recv[...].astype(F32)
        for z_ in range(8):
            rows = jnp.concatenate([by_quad[i, 8 * z_ : 8 * z_ + 8] for i in range(4)], axis=0)
            a2_send[z_] = rows.astype(BF16)
        for dz in range(1, 8):
            a2_copy(dz).start()
        a2_recv[z] = a2_send[z]

    def cap_partial():
        load_cap.wait()
        for dz in range(1, 8):
            a2_copy(dz).wait_recv()
        cap_rows = a2_recv[...].reshape(256, 128)
        for h in range(HEADS_HERE):
            product = jnp.dot(cap_rows, w_cap[h], preferred_element_type=F32)
            both = jnp.concatenate(
                [product[:, :128].reshape(8, 4, 8, 128), product[:, 128:].reshape(8, 4, 8, 128)],
                axis=2,
            )
            for i in range(4):
                part[i, :, :, h * 128 : (h + 1) * 128] = both[:, i].astype(BF16)
        r1_copy.start()

    def cap_cores():
        r1_copy.wait_recv()
        r2_send[...] = (part[c * 2 + other_xl].astype(F32) + r1_recv[other_xl].astype(F32)).astype(BF16)
        r2_copy.start()

    def cap_x():
        r2_copy.wait_recv()
        r3_send[...] = (
            part[quad].astype(F32) + r1_recv[xl].astype(F32) + r2_recv[...].astype(F32)
        ).astype(BF16)
        for dz in range(1, 8):
            r3_copy(dz).start()
        r3_recv[z] = r3_send[z]

    def cap_line():
        for dz in range(1, 8):
            r3_copy(dz).wait_recv()
        total = jnp.sum(r3_recv[...].astype(F32), axis=0)
        for h in range(HEADS_HERE):
            cols = slice(h * 128, (h + 1) * 128)
            key_rows = root_norm(total[0:8, cols], gains_ref[2:3, :]).astype(F32)
            cap_all[0, :, cols] = jnp.concatenate([key_rows, total[8:16, cols]], axis=0).astype(BF16)
        for dz in range(1, 8):
            capall_copy(dz).start()

    def forward_all(k, s):
        def head(h, carry):
            forward(k, h, s)
            return carry

        lax.fori_loop(0, HEADS_HERE, head, 0)

    def attend(h, slots, first=False, caption=None):
        q = q_buf[h].reshape(QUERIES, HEAD)
        keys = [jnp.concatenate([kv[h, s, k, 0] for k in range(PARTS)], axis=0) for s in slots]
        values = [jnp.concatenate([kv[h, s, k, 1] for k in range(PARTS)], axis=0) for s in slots]
        if caption is not None:
            keys.append(caption[0])
            values.append(caption[1])
        scores = [
            lax.dot_general(q, k, (((1,), (1,)), ((), ())), preferred_element_type=F32)
            for k in keys
        ]
        halves = [s[:, i : i + 128] for s in scores for i in range(0, s.shape[1], 128)]
        top = halves[0]
        for s in halves[1 : 2 * len(slots)]:
            top = jnp.maximum(top, s)
        top = jnp.max(top, axis=-1, keepdims=True)
        for s in halves[2 * len(slots) :]:
            top = jnp.maximum(top, jnp.max(s, axis=-1, keepdims=True))
        if first:
            m_new = jnp.broadcast_to(top, (QUERIES, 128))
        else:
            m_old = m_buf[h]
            m_new = jnp.maximum(m_old, top)
        wide = jnp.concatenate([m_new, m_new], axis=1)
        update = None
        for s, v in zip(scores, values):
            weights = jnp.exp2(s - wide[:, : s.shape[1]]).astype(BF16)
            filled = jnp.concatenate([v, jnp.ones(v.shape, BF16)], axis=1)
            term = jnp.dot(weights, filled, preferred_element_type=F32)
            update = term if update is None else update + term
        if first:
            acc[h] = update
        else:
            alpha = jnp.exp2(m_old - m_new)
            acc[h] = acc[h] * jnp.concatenate([alpha, alpha], axis=1) + update
        m_buf[h] = m_new

    token_onward(0)
    cap_columns()
    cap_partial()
    token_rest(0)
    token_near(1)
    load_qkv.wait()
    cap_cores()
    project(0)
    token_onward(1)
    cap_x()
    forward_all(0, 2)
    token_rest(1)
    project(1)
    cap_line()
    forward_all(1, 2)
    forward_all(0, 3)

    def step_three(h, carry):
        forward(1, h, 3)
        for j in range(1, 4):
            query_copy(h, j).wait_recv()
        attend(h, [0, 1, 7], first=True)
        return carry

    lax.fori_loop(0, HEADS_HERE, step_three, 0)

    forward_all(0, 4)
    for dz in range(1, 8):
        capall_copy(dz).wait_recv()

    def step_four(h, carry):
        forward(1, h, 4)
        col = pl.ds(pl.multiple_of(h * 128, 128), 128)
        cap_kv = cap_all[:, :, col].astype(F32)
        cap_keys = cap_kv[:, 0:8, :].reshape(64, 128).astype(BF16)
        cap_values = cap_kv[:, 8:16, :].reshape(64, 128).astype(BF16)
        attend(h, [2, 6], caption=(cap_keys, cap_values))
        attend(h, [3, 5])
        return carry

    lax.fori_loop(0, HEADS_HERE, step_four, 0)

    def core_copy(h):
        return pltpu.make_async_remote_copy(
            src_ref=o_send.at[h], dst_ref=o_recv.at[h],
            send_sem=o_ssem.at[h, 0], recv_sem=o_rsem.at[h, 0],
            device_id=quad_peer(1), device_id_type=MESH,
        )

    def core_level_copy(h):
        return pltpu.make_async_remote_copy(
            src_ref=l_send.at[h], dst_ref=l_recv.at[h],
            send_sem=o_ssem.at[h, 1], recv_sem=o_rsem.at[h, 1],
            device_id=quad_peer(1), device_id_type=MESH,
        )

    def x_copy(h):
        return pltpu.make_async_remote_copy(
            src_ref=ox_send.at[h], dst_ref=ox_recv.at[h],
            send_sem=o_ssem.at[h, 2], recv_sem=o_rsem.at[h, 2],
            device_id=quad_peer(2), device_id_type=MESH,
        )

    def x_level_copy(h):
        return pltpu.make_async_remote_copy(
            src_ref=lx_send.at[h], dst_ref=lx_recv.at[h],
            send_sem=o_ssem.at[h, 3], recv_sem=o_rsem.at[h, 3],
            device_id=quad_peer(2), device_id_type=MESH,
        )

    def partial_output(h, j):
        rows = slice(j * BLOCK, (j + 1) * BLOCK)
        denominator = acc[h, rows, 128:]
        return acc[h, rows, :128] / denominator, m_buf[h, rows, :] + jnp.log(denominator) * LOG2E

    def wide_level(level):
        return jnp.broadcast_to(level[0:1, :], (128, BLOCK)).T

    def merge(terms):
        top = terms[0][1]
        for _, level in terms[1:]:
            top = jnp.maximum(top, level)
        numerator, weight = None, None
        for out, level in terms:
            share = jnp.exp2(level - top)
            numerator = out * share if numerator is None else numerator + out * share
            weight = share if weight is None else weight + share
        return (numerator / weight).astype(BF16), top, weight

    def step_last(h):
        for k in range(PARTS):
            ring_right(k, h, 4).wait_recv()
            ring_left(k, h, 4).wait_recv()
        attend(h, [4])
        for i, j in enumerate((1, 3)):
            out, level = partial_output(h, j)
            o_send[h, i] = out.astype(BF16)
            l_send[h, i] = level.T[0:8, :]
        core_copy(h).start()
        core_level_copy(h).start()

    def step_pair(h):
        core_copy(h).wait_recv()
        core_level_copy(h).wait_recv()
        out, top, weight = merge(
            [partial_output(h, 2), (o_recv[h, 1].astype(F32), wide_level(l_recv[h, 1]))]
        )
        ox_send[h] = out
        lx_send[h] = (top + jnp.log(weight) * LOG2E).T[0:8, :]
        x_copy(h).start()
        x_level_copy(h).start()

    for h in range(HEADS_HERE):
        step_last(h)
        if h > 0:
            step_pair(h - 1)
    step_pair(HEADS_HERE - 1)

    def combine(h, carry):
        x_copy(h).wait_recv()
        x_level_copy(h).wait_recv()
        att[h] = merge(
            [
                partial_output(h, 0),
                (o_recv[h, 0].astype(F32), wide_level(l_recv[h, 0])),
                (ox_recv[h].astype(F32), wide_level(lx_recv[h])),
            ]
        )[0]
        return carry

    lax.fori_loop(0, HEADS_HERE, combine, 0)

    load_out.wait()

    def p_copy(n, i):
        source, (dy, dx) = REDUCE_HOPS[i]
        return pltpu.make_async_remote_copy(
            src_ref=p_send.at[n, source], dst_ref=p_recv.at[n, i],
            send_sem=p_ssem.at[n, i], recv_sem=p_rsem.at[n, i],
            device_id={"ulysses": ulysses_peer(dy, dx)}, device_id_type=MESH,
        )

    def out_chunk(n, carry):
        cols = pl.ds(pl.multiple_of(n * CHUNK, 128), CHUNK)
        rows = jnp.concatenate([att[h] for h in range(HEADS_HERE)], axis=1)
        product = jnp.dot(rows, w_out[:, cols], preferred_element_type=F32)
        product = product.reshape(PARTS, 8, PART, CHUNK)
        for i in (5, 6, 7, 3):
            p_send[n, i] = product[:, i].reshape(ROWS, CHUNK).astype(BF16)
        for i in range(4):
            p_copy(n, i).start()
        for k, i in enumerate((0, 1, 2, 4)):
            p_keep[n, k] = product[:, i].reshape(ROWS, CHUNK)
        return carry

    lax.fori_loop(0, CHUNKS, out_chunk, 0)

    def pass_on(n, carry):
        for k, i in ((1, 0), (2, 1), (3, 2)):
            p_copy(n, i).wait_recv()
            source = REDUCE_HOPS[i + 4][0]
            p_send[n, source] = (p_keep[n, k] + p_recv[n, i].astype(F32)).astype(BF16)
            p_copy(n, i + 4).start()
        return carry

    lax.fori_loop(0, CHUNKS, pass_on, 0)

    def finish(n, carry):
        cols = pl.ds(pl.multiple_of(n * CHUNK, 128), CHUNK)
        for i in range(3, 7):
            p_copy(n, i).wait_recv()
        projection = p_keep[n, 0] + jnp.sum(p_recv[n, 3:7].astype(F32), axis=0)
        out_ref[:, cols] = (
            img_ref[:, cols].astype(F32) + mod_ref[2:3, cols] * projection
        ).astype(BF16)
        return carry

    lax.fori_loop(0, CHUNKS, finish, 0)

    for j in range(1, 4):
        a1_copy(j).wait_send()
    r1_copy.wait_send()
    r2_copy.wait_send()
    for dz in range(1, 8):
        a2_copy(dz).wait_send()
        r3_copy(dz).wait_send()
        capall_copy(dz).wait_send()
    for k in range(PARTS):
        for i in range(7):
            token_copy(k, i).wait_send()

    def drain_head(h, carry):
        for s in range(1, 5):
            for k in range(PARTS):
                ring_right(k, h, s).wait_send()
                ring_left(k, h, s).wait_send()
        for j in range(1, 4):
            query_copy(h, j).wait_send()
        core_copy(h).wait_send()
        core_level_copy(h).wait_send()
        x_copy(h).wait_send()
        x_level_copy(h).wait_send()
        return carry

    lax.fori_loop(0, HEADS_HERE, drain_head, 0)

    def drain_chunk(n, carry):
        for i in range(7):
            p_copy(n, i).wait_send()
        return carry

    lax.fori_loop(0, CHUNKS, drain_chunk, 0)


def per_device(
    image_tokens, text_tokens, modulation, text_modulation, norm_gains,
    qkv_weight, text_kv_weight, out_weight,
):
    qkv = jnp.transpose(qkv_weight, (1, 0, 2))
    tkv = jnp.transpose(text_kv_weight, (1, 0, 2))
    dma = pltpu.SemaphoreType.DMA
    vmem = pl.BlockSpec(memory_space=pltpu.VMEM)
    hbm = pl.BlockSpec(memory_space=pl.ANY)
    h3 = HEADS_HERE
    return pl.pallas_call(
        kernel,
        out_shape=jax.ShapeDtypeStruct((ROWS, D), BF16),
        in_specs=[hbm] * 8,
        out_specs=vmem,
        scratch_shapes=[
            pltpu.VMEM((ROWS, D), BF16),
            pltpu.VMEM((CAP_ROWS, D), BF16),
            pltpu.VMEM((3, D), F32),
            pltpu.VMEM((2, D), F32),
            pltpu.VMEM((3, HEAD), F32),
            pltpu.VMEM((h3, D, 384), BF16),
            pltpu.VMEM((h3, 128, 256), BF16),
            pltpu.VMEM((384, D), BF16),
            pltpu.VMEM((PARTS, 8, PART, D), BF16),
            pltpu.VMEM((4, 64, 128), BF16),
            pltpu.VMEM((4, 64, 128), BF16),
            pltpu.VMEM((8, 32, 128), BF16),
            pltpu.VMEM((8, 32, 128), BF16),
            pltpu.VMEM((4, 8, 16, 384), BF16),
            pltpu.VMEM((2, 8, 16, 384), BF16),
            pltpu.VMEM((8, 16, 384), BF16),
            pltpu.VMEM((8, 16, 384), BF16),
            pltpu.VMEM((8, 16, 384), BF16),
            pltpu.VMEM((8, 16, 384), BF16),
            pltpu.VMEM((8, 16, 384), BF16),
            pltpu.VMEM((h3, 4, PARTS, BLOCK // PARTS, 128), BF16),
            pltpu.VMEM((h3, 8, PARTS, 2, BLOCK // PARTS, 128), BF16),
            pltpu.VMEM((h3, QUERIES, 128), F32),
            pltpu.VMEM((h3, QUERIES, 256), F32),
            pltpu.VMEM((h3, 2, BLOCK, 128), BF16),
            pltpu.VMEM((h3, 2, BLOCK, 128), BF16),
            pltpu.VMEM((h3, 2, 8, BLOCK), F32),
            pltpu.VMEM((h3, 2, 8, BLOCK), F32),
            pltpu.VMEM((h3, BLOCK, 128), BF16),
            pltpu.VMEM((h3, BLOCK, 128), BF16),
            pltpu.VMEM((h3, 8, BLOCK), F32),
            pltpu.VMEM((h3, 8, BLOCK), F32),
            pltpu.VMEM((h3, BLOCK, 128), BF16),
            pltpu.VMEM((CHUNKS, 8, ROWS, CHUNK), BF16),
            pltpu.VMEM((CHUNKS, 7, ROWS, CHUNK), BF16),
            pltpu.VMEM((CHUNKS, 4, ROWS, CHUNK), F32),
            dma((8,)), dma((PARTS, 7)), dma((PARTS, 7)), dma((4, 8)), dma((4, 8)), dma((2, 8)),
            dma((h3, 4)), dma((h3, 4)),
            dma((PARTS, h3, 4)), dma((PARTS, h3, 4)), dma((PARTS, h3, 4)), dma((PARTS, h3, 4)),
            dma((h3, 4)), dma((h3, 4)),
            dma((CHUNKS, 7)), dma((CHUNKS, 7)),
        ],
        compiler_params=pltpu.CompilerParams(
            collective_id=0, has_side_effects=True, vmem_limit_bytes=60 * 1024 * 1024
        ),
        name="joint_attention",
    )(image_tokens, text_tokens, modulation, text_modulation, norm_gains, qkv, tkv, out_weight)


def solution(mesh):
    in_specs = (
        P(("blk", "ulysses"), None),
        P("blk", None),
        P(),
        P(),
        P(),
        P(None, "ulysses", None),
        P("blk", "ulysses", None),
        P("ulysses", None),
    )
    out_specs = P(("blk", "ulysses"), None)
    return jax.shard_map(
        per_device, mesh=mesh, in_specs=in_specs, out_specs=out_specs, check_vma=False
    )
```

```python
import math

import jax
import jax.numpy as jnp
from jax import lax
from jax.experimental import pallas as pl
from jax.experimental.pallas import tpu as pltpu
from jax.sharding import PartitionSpec as P

D = 3072
HEAD = 128
HEADS_HERE = 3
ROWS = 32
BLOCK = 256
PARTS = 2
PART = ROWS // PARTS
QUERIES = 1024
CAP_COLS = 96
CAP_ROWS = 8
CHUNKS = 4
CHUNK = D // CHUNKS
MESH = pl.DeviceIdType.MESH
F32 = jnp.float32
BF16 = jnp.bfloat16
QUERY_SCALE = math.log2(math.e) / math.sqrt(HEAD)
LOG2E = math.log2(math.e)
NEAR_STEPS = [(1, 0), (3, 0), (2, 0), (0, 1)]
TOKEN_HOPS = [
    (0, (1, 0)), (0, (3, 0)), (0, (2, 0)), (0, (0, 1)),
    (1, (0, 1)), (2, (0, 1)), (4, (2, 0)),
]
REDUCE_HOPS = [
    (5, (0, 1)), (6, (0, 1)), (7, (2, 0)), (3, (2, 0)),
    (1, (3, 0)), (2, (1, 0)), (4, (0, 1)),
]


def layer_norm(values, shift, scale):
    average = jnp.mean(values, axis=-1, keepdims=True)
    centered = values - average
    spread = jnp.mean(centered * centered, axis=-1, keepdims=True)
    return (centered * lax.rsqrt(spread + 1e-06) * (1.0 + scale) + shift).astype(BF16)


def root_norm(values, gain):
    squares = jnp.mean(values * values, axis=-1, keepdims=True)
    return (values * lax.rsqrt(squares + 1e-06) * gain).astype(BF16)


def kernel(
    img_hbm, text_hbm, mod_hbm, tmod_hbm, gains_hbm, qkv_hbm, tkv_hbm, out_hbm,
    out_ref,
    img_ref, text_ref, mod_ref, tmod_ref, gains_ref,
    w_qkv, w_cap, w_out, tok, a1_send, a1_recv, a2_send, a2_recv,
    part, r1_recv, r2_send, r2_recv, r3_send, r3_recv, cap_all,
    q_buf, kv, m_buf, acc, o_send, o_recv, l_send, l_recv, ox_send, ox_recv, lx_send, lx_recv, att, p_send, p_recv, p_keep,
    w_sem, tok_send, tok_recv, a_sems, r_sems, capall_sems,
    q_send, q_recv, right_send, right_recv, left_send, left_recv,
    o_ssem, o_rsem, p_ssem, p_rsem,
):
    u = lax.axis_index("ulysses")
    b = lax.axis_index("blk")
    y, xh = u // 2, lax.rem(u, 2)
    xl, z, c = b // 16, lax.rem(b // 2, 8), lax.rem(b, 2)

    def ulysses_peer(dy, dx):
        return lax.rem(y + dy, 4) * 2 + lax.rem(xh + dx, 2)

    def blk_of(xl_, z_, c_):
        return xl_ * 16 + z_ * 2 + c_

    def quad_peer(j):
        return {"blk": blk_of(lax.rem(xl + j // 2, 2), z, lax.rem(c + j % 2, 2))}

    def line_peer(dz):
        return {"blk": blk_of(xl, lax.rem(z + dz, 8), c)}

    load_cap = pltpu.make_async_copy(tkv_hbm, w_cap.at[:, pl.ds(0, CAP_COLS), :], w_sem.at[0])
    load_qkv = pltpu.make_async_copy(qkv_hbm, w_qkv, w_sem.at[1])
    load_out = pltpu.make_async_copy(out_hbm, w_out, w_sem.at[2])
    small = [
        pltpu.make_async_copy(src, dst, w_sem.at[3 + i])
        for i, (src, dst) in enumerate(
            [
                (img_hbm, img_ref),
                (mod_hbm, mod_ref),
                (text_hbm, text_ref),
                (tmod_hbm, tmod_ref),
                (gains_hbm, gains_ref),
            ]
        )
    ]
    for load in small:
        load.start()
    load_cap.start()
    load_qkv.start()
    load_out.start()

    barrier = pltpu.get_barrier_semaphore()
    for dy, dx in NEAR_STEPS:
        pl.semaphore_signal(
            barrier, inc=1, device_id={"ulysses": ulysses_peer(dy, dx)}, device_id_type=MESH
        )

    for j in range(1, 4):
        pl.semaphore_signal(barrier, inc=1, device_id=quad_peer(j), device_id_type=MESH)
    for dz in range(1, 8):
        pl.semaphore_signal(barrier, inc=1, device_id=line_peer(dz), device_id_type=MESH)

    small[0].wait()
    small[1].wait()
    normed = layer_norm(img_ref[...].astype(F32), mod_ref[0:1, :], mod_ref[1:2, :])
    for k in range(PARTS):
        tok[k, 0] = normed[k * PART : (k + 1) * PART]

    pl.semaphore_wait(barrier, 14)

    quad = c * 2 + xl

    def a1_copy(j):
        to = lax.rem(c + j % 2, 2) * 2 + lax.rem(xl + j // 2, 2)
        return pltpu.make_async_remote_copy(
            src_ref=a1_send.at[to], dst_ref=a1_recv.at[quad],
            send_sem=a_sems.at[0, j], recv_sem=a_sems.at[1, j],
            device_id=quad_peer(j), device_id_type=MESH,
        )

    def a2_copy(dz):
        return pltpu.make_async_remote_copy(
            src_ref=a2_send.at[lax.rem(z + dz, 8)], dst_ref=a2_recv.at[z],
            send_sem=a_sems.at[2, dz], recv_sem=a_sems.at[3, dz],
            device_id=line_peer(dz), device_id_type=MESH,
        )

    def token_copy(k, i):
        source, (dy, dx) = TOKEN_HOPS[i]
        return pltpu.make_async_remote_copy(
            src_ref=tok.at[k, source], dst_ref=tok.at[k, i + 1],
            send_sem=tok_send.at[k, i], recv_sem=tok_recv.at[k, i],
            device_id={"ulysses": ulysses_peer(dy, dx)}, device_id_type=MESH,
        )

    def token_near(k):
        for i in (3, 0, 1):
            token_copy(k, i).start()

    def token_onward(k):
        for source, onward in ((0, 4), (1, 5), (3, 6)):
            token_copy(k, source).wait_recv()
            token_copy(k, onward).start()
        token_copy(k, 2).start()

    def token_rest(k):
        for i in (2, 4, 5, 6):
            token_copy(k, i).wait_recv()

    token_near(0)

    for load in small[2:]:
        load.wait()
    cap = layer_norm(text_ref[...].astype(F32), tmod_ref[0:1, :], tmod_ref[1:2, :]).astype(F32)
    groups = jnp.concatenate([cap[:, 384 * g : 384 * g + 384] for g in range(8)], axis=0)
    row = lax.broadcasted_iota(jnp.int32, (384, 512), 0)
    col = lax.broadcasted_iota(jnp.int32, (384, 512), 1)
    lane = col & 127
    pick = jnp.where((lane < CAP_COLS) & (row == (col >> 7) * CAP_COLS + lane), 1.0, 0.0)
    pieces = jnp.dot(groups.astype(BF16), pick.astype(BF16), preferred_element_type=F32)

    def piece(xl_, z_, c_):
        g, t = divmod(xl_ * 16 + z_ * 2 + c_, 4)
        return pieces[8 * g : 8 * g + 8, 128 * t : 128 * t + 128]

    for c_ in range(2):
        for xl_ in range(2):
            rows = jnp.concatenate([piece(xl_, z_, c_) for z_ in range(8)], axis=0)
            a1_send[c_ * 2 + xl_] = rows.astype(BF16)
    for h in range(HEADS_HERE):
        w_cap[h, CAP_COLS:128, :] = jnp.zeros((128 - CAP_COLS, 256), BF16)
    for j in range(1, 4):
        a1_copy(j).start()

    other_c, other_xl = lax.rem(c + 1, 2), lax.rem(xl + 1, 2)
    r1_copy = pltpu.make_async_remote_copy(
        src_ref=part.at[pl.ds(other_c * 2, 2)], dst_ref=r1_recv,
        send_sem=r_sems.at[0, 0], recv_sem=r_sems.at[1, 0],
        device_id=quad_peer(1), device_id_type=MESH,
    )
    r2_copy = pltpu.make_async_remote_copy(
        src_ref=r2_send, dst_ref=r2_recv,
        send_sem=r_sems.at[0, 1], recv_sem=r_sems.at[1, 1],
        device_id=quad_peer(2), device_id_type=MESH,
    )

    def r3_copy(dz):
        return pltpu.make_async_remote_copy(
            src_ref=r3_send.at[lax.rem(z + dz, 8)], dst_ref=r3_recv.at[z],
            send_sem=r_sems.at[2, dz], recv_sem=r_sems.at[3, dz],
            device_id=line_peer(dz), device_id_type=MESH,
        )

    def capall_copy(dz):
        return pltpu.make_async_remote_copy(
            src_ref=cap_all.at[0], dst_ref=cap_all.at[dz],
            send_sem=capall_sems.at[0, dz], recv_sem=capall_sems.at[1, dz],
            device_id=line_peer(dz), device_id_type=MESH,
        )

    def ring_right(k, h, s):
        src, dst = kv.at[h, s - 1, k], kv.at[h, s, k]
        if s == 4:
            src, dst = src.at[0], dst.at[0]
        return pltpu.make_async_remote_copy(
            src_ref=src, dst_ref=dst, send_sem=right_send.at[k, h, s - 1],
            recv_sem=right_recv.at[k, h, s - 1], device_id=line_peer(1), device_id_type=MESH,
        )

    def ring_left(k, h, s):
        src, dst = kv.at[h, (9 - s) % 8, k], kv.at[h, 8 - s, k]
        if s == 4:
            src, dst = src.at[1], dst.at[1]
        return pltpu.make_async_remote_copy(
            src_ref=src, dst_ref=dst, send_sem=left_send.at[k, h, s - 1],
            recv_sem=left_recv.at[k, h, s - 1], device_id=line_peer(7), device_id_type=MESH,
        )

    def query_copy(h, j):
        return pltpu.make_async_remote_copy(
            src_ref=q_buf.at[h, 2 if j == 3 else 0], dst_ref=q_buf.at[h, j],
            send_sem=q_send.at[h, j], recv_sem=q_recv.at[h, j],
            device_id=quad_peer(2 if j == 2 else 1), device_id_type=MESH,
        )

    def query_onward():
        def head(h, carry):
            query_copy(h, 2).wait_recv()
            query_copy(h, 3).start()
            return carry

        lax.fori_loop(0, HEADS_HERE, head, 0)

    def forward(k, h, s):
        ring_right(k, h, s - 1).wait_recv()
        ring_right(k, h, s).start()
        ring_left(k, h, s - 1).wait_recv()
        ring_left(k, h, s).start()

    def project(k):
        def head(h, carry):
            rows = tok[k].reshape(PART * 8, D)
            projected = jnp.dot(rows, w_qkv[h], preferred_element_type=F32)
            kv[h, 0, k, 0] = root_norm(projected[:, 128:256], gains_ref[1:2, :])
            kv[h, 0, k, 1] = projected[:, 256:384].astype(BF16)
            ring_right(k, h, 1).start()
            ring_left(k, h, 1).start()
            q_buf[h, 0, k] = root_norm(projected[:, 0:128], gains_ref[0:1, :] * QUERY_SCALE)
            if k == PARTS - 1:
                for j in (2, 1):
                    query_copy(h, j).start()
            return carry

        lax.fori_loop(0, HEADS_HERE, head, 0)

    def cap_columns():
        a1_recv[quad] = a1_send[quad]
        for j in range(1, 4):
            a1_copy(j).wait_recv()
        by_quad = a1_recv[...].astype(F32)
        for z_ in range(8):
            rows = jnp.concatenate([by_quad[i, 8 * z_ : 8 * z_ + 8] for i in range(4)], axis=0)
            a2_send[z_] = rows.astype(BF16)
        for dz in range(1, 8):
            a2_copy(dz).start()
        a2_recv[z] = a2_send[z]

    def cap_partial():
        load_cap.wait()
        for dz in range(1, 8):
            a2_copy(dz).wait_recv()
        cap_rows = a2_recv[...].reshape(256, 128)
        for h in range(HEADS_HERE):
            product = jnp.dot(cap_rows, w_cap[h], preferred_element_type=F32)
            both = jnp.concatenate(
                [product[:, :128].reshape(8, 4, 8, 128), product[:, 128:].reshape(8, 4, 8, 128)],
                axis=2,
            )
            for i in range(4):
                part[i, :, :, h * 128 : (h + 1) * 128] = both[:, i].astype(BF16)
        r1_copy.start()

    def cap_cores():
        r1_copy.wait_recv()
        r2_send[...] = (part[c * 2 + other_xl].astype(F32) + r1_recv[other_xl].astype(F32)).astype(BF16)
        r2_copy.start()

    def cap_x():
        r2_copy.wait_recv()
        r3_send[...] = (
            part[quad].astype(F32) + r1_recv[xl].astype(F32) + r2_recv[...].astype(F32)
        ).astype(BF16)
        for dz in range(1, 8):
            r3_copy(dz).start()
        r3_recv[z] = r3_send[z]

    def cap_line():
        for dz in range(1, 8):
            r3_copy(dz).wait_recv()
        total = jnp.sum(r3_recv[...].astype(F32), axis=0)
        for h in range(HEADS_HERE):
            cols = slice(h * 128, (h + 1) * 128)
            key_rows = root_norm(total[0:8, cols], gains_ref[2:3, :]).astype(F32)
            cap_all[0, :, cols] = jnp.concatenate([key_rows, total[8:16, cols]], axis=0).astype(BF16)
        for dz in range(1, 8):
            capall_copy(dz).start()

    def forward_all(k, s):
        def head(h, carry):
            forward(k, h, s)
            return carry

        lax.fori_loop(0, HEADS_HERE, head, 0)

    def attend(h, slots, first=False, caption=None):
        q = q_buf[h].reshape(QUERIES, HEAD)
        keys = [jnp.concatenate([kv[h, s, k, 0] for k in range(PARTS)], axis=0) for s in slots]
        values = [jnp.concatenate([kv[h, s, k, 1] for k in range(PARTS)], axis=0) for s in slots]
        if caption is not None:
            keys.append(caption[0])
            values.append(caption[1])
        scores = [
            lax.dot_general(q, k, (((1,), (1,)), ((), ())), preferred_element_type=F32)
            for k in keys
        ]
        halves = [s[:, i : i + 128] for s in scores for i in range(0, s.shape[1], 128)]
        top = halves[0]
        for s in halves[1 : 2 * len(slots)]:
            top = jnp.maximum(top, s)
        top = jnp.max(top, axis=-1, keepdims=True)
        for s in halves[2 * len(slots) :]:
            top = jnp.maximum(top, jnp.max(s, axis=-1, keepdims=True))
        if first:
            m_new = jnp.broadcast_to(top, (QUERIES, 128))
        else:
            m_old = m_buf[h]
            m_new = jnp.maximum(m_old, top)
        wide = jnp.concatenate([m_new, m_new], axis=1)
        update = None
        for s, v in zip(scores, values):
            weights = jnp.exp2(s - wide[:, : s.shape[1]]).astype(BF16)
            filled = jnp.concatenate([v, jnp.ones(v.shape, BF16)], axis=1)
            term = jnp.dot(weights, filled, preferred_element_type=F32)
            update = term if update is None else update + term
        if first:
            acc[h] = update
        else:
            alpha = jnp.exp2(m_old - m_new)
            acc[h] = acc[h] * jnp.concatenate([alpha, alpha], axis=1) + update
        m_buf[h] = m_new

    token_onward(0)
    cap_columns()
    cap_partial()
    token_rest(0)
    token_near(1)
    load_qkv.wait()
    cap_cores()
    project(0)
    token_onward(1)
    cap_x()
    forward_all(0, 2)
    token_rest(1)
    project(1)
    cap_line()
    forward_all(1, 2)
    query_onward()
    forward_all(0, 3)

    def step_three(h, carry):
        forward(1, h, 3)
        for j in (1, 3):
            query_copy(h, j).wait_recv()
        attend(h, [0, 1], first=True)
        attend(h, [7, 2])
        return carry

    lax.fori_loop(0, HEADS_HERE, step_three, 0)

    forward_all(0, 4)
    for dz in range(1, 8):
        capall_copy(dz).wait_recv()

    def step_four(h, carry):
        forward(1, h, 4)
        col = pl.ds(pl.multiple_of(h * 128, 128), 128)
        cap_kv = cap_all[:, :, col].astype(F32)
        cap_keys = cap_kv[:, 0:8, :].reshape(64, 128).astype(BF16)
        cap_values = cap_kv[:, 8:16, :].reshape(64, 128).astype(BF16)
        attend(h, [6, 3])
        attend(h, [5], caption=(cap_keys, cap_values))
        return carry

    lax.fori_loop(0, HEADS_HERE, step_four, 0)

    def core_copy(h):
        return pltpu.make_async_remote_copy(
            src_ref=o_send.at[h], dst_ref=o_recv.at[h],
            send_sem=o_ssem.at[h, 0], recv_sem=o_rsem.at[h, 0],
            device_id=quad_peer(1), device_id_type=MESH,
        )

    def core_level_copy(h):
        return pltpu.make_async_remote_copy(
            src_ref=l_send.at[h], dst_ref=l_recv.at[h],
            send_sem=o_ssem.at[h, 1], recv_sem=o_rsem.at[h, 1],
            device_id=quad_peer(1), device_id_type=MESH,
        )

    def x_copy(h):
        return pltpu.make_async_remote_copy(
            src_ref=ox_send.at[h], dst_ref=ox_recv.at[h],
            send_sem=o_ssem.at[h, 2], recv_sem=o_rsem.at[h, 2],
            device_id=quad_peer(2), device_id_type=MESH,
        )

    def x_level_copy(h):
        return pltpu.make_async_remote_copy(
            src_ref=lx_send.at[h], dst_ref=lx_recv.at[h],
            send_sem=o_ssem.at[h, 3], recv_sem=o_rsem.at[h, 3],
            device_id=quad_peer(2), device_id_type=MESH,
        )

    def partial_output(h, j):
        rows = slice(j * BLOCK, (j + 1) * BLOCK)
        denominator = acc[h, rows, 128:]
        return acc[h, rows, :128] / denominator, m_buf[h, rows, :] + jnp.log(denominator) * LOG2E

    def wide_level(level):
        return jnp.broadcast_to(level[0:1, :], (128, BLOCK)).T

    def merge(terms):
        top = terms[0][1]
        for _, level in terms[1:]:
            top = jnp.maximum(top, level)
        numerator, weight = None, None
        for out, level in terms:
            share = jnp.exp2(level - top)
            numerator = out * share if numerator is None else numerator + out * share
            weight = share if weight is None else weight + share
        return (numerator / weight).astype(BF16), top, weight

    def step_last(h):
        for k in range(PARTS):
            ring_right(k, h, 4).wait_recv()
            ring_left(k, h, 4).wait_recv()
        attend(h, [4])
        for i, j in enumerate((1, 3)):
            out, level = partial_output(h, j)
            o_send[h, i] = out.astype(BF16)
            l_send[h, i] = level.T[0:8, :]
        core_copy(h).start()
        core_level_copy(h).start()

    def step_pair(h):
        core_copy(h).wait_recv()
        core_level_copy(h).wait_recv()
        out, top, weight = merge(
            [partial_output(h, 2), (o_recv[h, 1].astype(F32), wide_level(l_recv[h, 1]))]
        )
        ox_send[h] = out
        lx_send[h] = (top + jnp.log(weight) * LOG2E).T[0:8, :]
        x_copy(h).start()
        x_level_copy(h).start()

    def last_loop(h, carry):
        step_last(h)
        return carry

    lax.fori_loop(0, HEADS_HERE, last_loop, 0)

    def pair_loop(h, carry):
        step_pair(h)
        return carry

    lax.fori_loop(0, HEADS_HERE, pair_loop, 0)

    def combine(h, carry):
        x_copy(h).wait_recv()
        x_level_copy(h).wait_recv()
        att[h] = merge(
            [
                partial_output(h, 0),
                (o_recv[h, 0].astype(F32), wide_level(l_recv[h, 0])),
                (ox_recv[h].astype(F32), wide_level(lx_recv[h])),
            ]
        )[0]
        return carry

    lax.fori_loop(0, HEADS_HERE, combine, 0)

    load_out.wait()

    def p_copy(n, i):
        source, (dy, dx) = REDUCE_HOPS[i]
        return pltpu.make_async_remote_copy(
            src_ref=p_send.at[n, source], dst_ref=p_recv.at[n, i],
            send_sem=p_ssem.at[n, i], recv_sem=p_rsem.at[n, i],
            device_id={"ulysses": ulysses_peer(dy, dx)}, device_id_type=MESH,
        )

    def out_chunk(n, carry):
        cols = pl.ds(pl.multiple_of(n * CHUNK, 128), CHUNK)
        rows = jnp.concatenate([att[h] for h in range(HEADS_HERE)], axis=1)
        product = jnp.dot(rows, w_out[:, cols], preferred_element_type=F32)
        product = product.reshape(PARTS, 8, PART, CHUNK)
        for i in (5, 6, 7, 3):
            p_send[n, i] = product[:, i].reshape(ROWS, CHUNK).astype(BF16)
        for i in range(4):
            p_copy(n, i).start()
        for k, i in enumerate((0, 1, 2, 4)):
            p_keep[n, k] = product[:, i].reshape(ROWS, CHUNK)
        return carry

    lax.fori_loop(0, CHUNKS, out_chunk, 0)

    def pass_on(n, carry):
        for k, i in ((1, 0), (2, 1), (3, 2)):
            p_copy(n, i).wait_recv()
            source = REDUCE_HOPS[i + 4][0]
            p_send[n, source] = (p_keep[n, k] + p_recv[n, i].astype(F32)).astype(BF16)
            p_copy(n, i + 4).start()
        return carry

    lax.fori_loop(0, CHUNKS, pass_on, 0)

    def finish(n, carry):
        cols = pl.ds(pl.multiple_of(n * CHUNK, 128), CHUNK)
        for i in range(3, 7):
            p_copy(n, i).wait_recv()
        projection = p_keep[n, 0] + jnp.sum(p_recv[n, 3:7].astype(F32), axis=0)
        out_ref[:, cols] = (
            img_ref[:, cols].astype(F32) + mod_ref[2:3, cols] * projection
        ).astype(BF16)
        return carry

    lax.fori_loop(0, CHUNKS, finish, 0)

    for j in range(1, 4):
        a1_copy(j).wait_send()
    r1_copy.wait_send()
    r2_copy.wait_send()
    for dz in range(1, 8):
        a2_copy(dz).wait_send()
        r3_copy(dz).wait_send()
        capall_copy(dz).wait_send()
    for k in range(PARTS):
        for i in range(7):
            token_copy(k, i).wait_send()

    def drain_head(h, carry):
        for s in range(1, 5):
            for k in range(PARTS):
                ring_right(k, h, s).wait_send()
                ring_left(k, h, s).wait_send()
        for j in range(1, 4):
            query_copy(h, j).wait_send()
        core_copy(h).wait_send()
        core_level_copy(h).wait_send()
        x_copy(h).wait_send()
        x_level_copy(h).wait_send()
        return carry

    lax.fori_loop(0, HEADS_HERE, drain_head, 0)

    def drain_chunk(n, carry):
        for i in range(7):
            p_copy(n, i).wait_send()
        return carry

    lax.fori_loop(0, CHUNKS, drain_chunk, 0)


def per_device(
    image_tokens, text_tokens, modulation, text_modulation, norm_gains,
    qkv_weight, text_kv_weight, out_weight,
):
    qkv = jnp.transpose(qkv_weight, (1, 0, 2))
    tkv = jnp.transpose(text_kv_weight, (1, 0, 2))
    dma = pltpu.SemaphoreType.DMA
    vmem = pl.BlockSpec(memory_space=pltpu.VMEM)
    hbm = pl.BlockSpec(memory_space=pl.ANY)
    h3 = HEADS_HERE
    return pl.pallas_call(
        kernel,
        out_shape=jax.ShapeDtypeStruct((ROWS, D), BF16),
        in_specs=[hbm] * 8,
        out_specs=vmem,
        scratch_shapes=[
            pltpu.VMEM((ROWS, D), BF16),
            pltpu.VMEM((CAP_ROWS, D), BF16),
            pltpu.VMEM((3, D), F32),
            pltpu.VMEM((2, D), F32),
            pltpu.VMEM((3, HEAD), F32),
            pltpu.VMEM((h3, D, 384), BF16),
            pltpu.VMEM((h3, 128, 256), BF16),
            pltpu.VMEM((384, D), BF16),
            pltpu.VMEM((PARTS, 8, PART, D), BF16),
            pltpu.VMEM((4, 64, 128), BF16),
            pltpu.VMEM((4, 64, 128), BF16),
            pltpu.VMEM((8, 32, 128), BF16),
            pltpu.VMEM((8, 32, 128), BF16),
            pltpu.VMEM((4, 8, 16, 384), BF16),
            pltpu.VMEM((2, 8, 16, 384), BF16),
            pltpu.VMEM((8, 16, 384), BF16),
            pltpu.VMEM((8, 16, 384), BF16),
            pltpu.VMEM((8, 16, 384), BF16),
            pltpu.VMEM((8, 16, 384), BF16),
            pltpu.VMEM((8, 16, 384), BF16),
            pltpu.VMEM((h3, 4, PARTS, BLOCK // PARTS, 128), BF16),
            pltpu.VMEM((h3, 8, PARTS, 2, BLOCK // PARTS, 128), BF16),
            pltpu.VMEM((h3, QUERIES, 128), F32),
            pltpu.VMEM((h3, QUERIES, 256), F32),
            pltpu.VMEM((h3, 2, BLOCK, 128), BF16),
            pltpu.VMEM((h3, 2, BLOCK, 128), BF16),
            pltpu.VMEM((h3, 2, 8, BLOCK), F32),
            pltpu.VMEM((h3, 2, 8, BLOCK), F32),
            pltpu.VMEM((h3, BLOCK, 128), BF16),
            pltpu.VMEM((h3, BLOCK, 128), BF16),
            pltpu.VMEM((h3, 8, BLOCK), F32),
            pltpu.VMEM((h3, 8, BLOCK), F32),
            pltpu.VMEM((h3, BLOCK, 128), BF16),
            pltpu.VMEM((CHUNKS, 8, ROWS, CHUNK), BF16),
            pltpu.VMEM((CHUNKS, 7, ROWS, CHUNK), BF16),
            pltpu.VMEM((CHUNKS, 4, ROWS, CHUNK), F32),
            dma((8,)), dma((PARTS, 7)), dma((PARTS, 7)), dma((4, 8)), dma((4, 8)), dma((2, 8)),
            dma((h3, 4)), dma((h3, 4)),
            dma((PARTS, h3, 4)), dma((PARTS, h3, 4)), dma((PARTS, h3, 4)), dma((PARTS, h3, 4)),
            dma((h3, 4)), dma((h3, 4)),
            dma((CHUNKS, 7)), dma((CHUNKS, 7)),
        ],
        compiler_params=pltpu.CompilerParams(
            collective_id=0, has_side_effects=True, vmem_limit_bytes=60 * 1024 * 1024
        ),
        name="joint_attention",
    )(image_tokens, text_tokens, modulation, text_modulation, norm_gains, qkv, tkv, out_weight)


def solution(mesh):
    in_specs = (
        P(("blk", "ulysses"), None),
        P("blk", None),
        P(),
        P(),
        P(),
        P(None, "ulysses", None),
        P("blk", "ulysses", None),
        P("ulysses", None),
    )
    out_specs = P(("blk", "ulysses"), None)
    return jax.shard_map(
        per_device, mesh=mesh, in_specs=in_specs, out_specs=out_specs, check_vma=False
    )
```

```python
import math

import jax
import jax.numpy as jnp
from jax import lax
from jax.experimental import pallas as pl
from jax.experimental.pallas import tpu as pltpu
from jax.sharding import PartitionSpec as P

D = 3072
HEAD = 128
HEADS_HERE = 3
ROWS = 32
BLOCK = 256
PARTS = 2
PART = ROWS // PARTS
QUERIES = 1024
CAP_COLS = 96
CAP_ROWS = 8
CHUNKS = 4
CHUNK = D // CHUNKS
MESH = pl.DeviceIdType.MESH
F32 = jnp.float32
BF16 = jnp.bfloat16
QUERY_SCALE = math.log2(math.e) / math.sqrt(HEAD)
LOG2E = math.log2(math.e)
NEAR_STEPS = [(1, 0), (3, 0), (2, 0), (0, 1)]
TOKEN_HOPS = [
    (0, (1, 0)), (0, (3, 0)), (0, (2, 0)), (0, (0, 1)),
    (1, (0, 1)), (2, (0, 1)), (4, (2, 0)),
]
REDUCE_HOPS = [
    (5, (0, 1)), (6, (0, 1)), (7, (2, 0)), (3, (2, 0)),
    (1, (3, 0)), (2, (1, 0)), (4, (0, 1)),
]


def layer_norm(values, shift, scale):
    average = jnp.mean(values, axis=-1, keepdims=True)
    centered = values - average
    spread = jnp.mean(centered * centered, axis=-1, keepdims=True)
    return (centered * lax.rsqrt(spread + 1e-06) * (1.0 + scale) + shift).astype(BF16)


def root_norm(values, gain):
    squares = jnp.mean(values * values, axis=-1, keepdims=True)
    return (values * lax.rsqrt(squares + 1e-06) * gain).astype(BF16)


def kernel(
    img_hbm, text_hbm, mod_hbm, tmod_hbm, gains_hbm, qkv_hbm, tkv_hbm, out_hbm,
    out_ref,
    img_ref, text_ref, mod_ref, tmod_ref, gains_ref,
    w_qkv, w_cap, w_out, tok, a1_send, a1_recv, a2_send, a2_recv,
    part, r1_recv, r2_send, r2_recv, r3_send, r3_recv, cap_all,
    q_buf, kv, m_buf, acc, o_send, o_recv, l_send, l_recv, ox_send, ox_recv, lx_send, lx_recv, att, p_send, p_recv, p_keep,
    w_sem, tok_send, tok_recv, a_sems, r_sems, capall_sems,
    q_send, q_recv, right_send, right_recv, left_send, left_recv,
    o_ssem, o_rsem, p_ssem, p_rsem,
):
    u = lax.axis_index("ulysses")
    b = lax.axis_index("blk")
    y, xh = u // 2, lax.rem(u, 2)
    xl, z, c = b // 16, lax.rem(b // 2, 8), lax.rem(b, 2)

    def ulysses_peer(dy, dx):
        return lax.rem(y + dy, 4) * 2 + lax.rem(xh + dx, 2)

    def blk_of(xl_, z_, c_):
        return xl_ * 16 + z_ * 2 + c_

    def quad_peer(j):
        return {"blk": blk_of(lax.rem(xl + j // 2, 2), z, lax.rem(c + j % 2, 2))}

    def line_peer(dz):
        return {"blk": blk_of(xl, lax.rem(z + dz, 8), c)}

    barrier = pltpu.get_barrier_semaphore()
    for dy, dx in NEAR_STEPS:
        pl.semaphore_signal(
            barrier, inc=1, device_id={"ulysses": ulysses_peer(dy, dx)}, device_id_type=MESH
        )

    for j in range(1, 4):
        pl.semaphore_signal(barrier, inc=1, device_id=quad_peer(j), device_id_type=MESH)
    for dz in range(1, 8):
        pl.semaphore_signal(barrier, inc=1, device_id=line_peer(dz), device_id_type=MESH)

    load_cap = pltpu.make_async_copy(tkv_hbm, w_cap.at[:, pl.ds(0, CAP_COLS), :], w_sem.at[0])
    load_qkv = pltpu.make_async_copy(qkv_hbm, w_qkv, w_sem.at[1])
    load_out = pltpu.make_async_copy(out_hbm, w_out, w_sem.at[2])
    small = [
        pltpu.make_async_copy(src, dst, w_sem.at[3 + i])
        for i, (src, dst) in enumerate(
            [
                (img_hbm, img_ref),
                (mod_hbm, mod_ref),
                (text_hbm, text_ref),
                (tmod_hbm, tmod_ref),
                (gains_hbm, gains_ref),
            ]
        )
    ]
    for load in small:
        load.start()
    load_cap.start()
    load_qkv.start()
    load_out.start()

    small[0].wait()
    small[1].wait()
    normed = layer_norm(img_ref[...].astype(F32), mod_ref[0:1, :], mod_ref[1:2, :])
    for k in range(PARTS):
        tok[k, 0] = normed[k * PART : (k + 1) * PART]

    pl.semaphore_wait(barrier, 14)

    quad = c * 2 + xl

    def a1_copy(j):
        to = lax.rem(c + j % 2, 2) * 2 + lax.rem(xl + j // 2, 2)
        return pltpu.make_async_remote_copy(
            src_ref=a1_send.at[to], dst_ref=a1_recv.at[quad],
            send_sem=a_sems.at[0, j], recv_sem=a_sems.at[1, j],
            device_id=quad_peer(j), device_id_type=MESH,
        )

    def a2_copy(dz):
        return pltpu.make_async_remote_copy(
            src_ref=a2_send.at[lax.rem(z + dz, 8)], dst_ref=a2_recv.at[z],
            send_sem=a_sems.at[2, dz], recv_sem=a_sems.at[3, dz],
            device_id=line_peer(dz), device_id_type=MESH,
        )

    def token_copy(k, i):
        source, (dy, dx) = TOKEN_HOPS[i]
        return pltpu.make_async_remote_copy(
            src_ref=tok.at[k, source], dst_ref=tok.at[k, i + 1],
            send_sem=tok_send.at[k, i], recv_sem=tok_recv.at[k, i],
            device_id={"ulysses": ulysses_peer(dy, dx)}, device_id_type=MESH,
        )

    def token_near(k):
        for i in (3, 0, 1):
            token_copy(k, i).start()

    def token_onward(k):
        for source, onward in ((0, 4), (1, 5)):
            token_copy(k, source).wait_recv()
            token_copy(k, onward).start()
        token_copy(k, 2).start()
        token_copy(k, 3).wait_recv()
        token_copy(k, 6).start()

    def token_rest(k):
        for i in (2, 4, 5, 6):
            token_copy(k, i).wait_recv()

    token_near(0)

    for load in small[2:]:
        load.wait()
    cap = layer_norm(text_ref[...].astype(F32), tmod_ref[0:1, :], tmod_ref[1:2, :]).astype(F32)
    groups = jnp.concatenate([cap[:, 384 * g : 384 * g + 384] for g in range(8)], axis=0)
    row = lax.broadcasted_iota(jnp.int32, (384, 512), 0)
    col = lax.broadcasted_iota(jnp.int32, (384, 512), 1)
    lane = col & 127
    pick = jnp.where((lane < CAP_COLS) & (row == (col >> 7) * CAP_COLS + lane), 1.0, 0.0)
    pieces = jnp.dot(groups.astype(BF16), pick.astype(BF16), preferred_element_type=F32)

    def piece(xl_, z_, c_):
        g, t = divmod(xl_ * 16 + z_ * 2 + c_, 4)
        return pieces[8 * g : 8 * g + 8, 128 * t : 128 * t + 128]

    for c_ in range(2):
        for xl_ in range(2):
            rows = jnp.concatenate([piece(xl_, z_, c_) for z_ in range(8)], axis=0)
            a1_send[c_ * 2 + xl_] = rows.astype(BF16)
    for h in range(HEADS_HERE):
        w_cap[h, CAP_COLS:128, :] = jnp.zeros((128 - CAP_COLS, 256), BF16)
    for j in range(1, 4):
        a1_copy(j).start()

    other_c, other_xl = lax.rem(c + 1, 2), lax.rem(xl + 1, 2)
    r1_copy = pltpu.make_async_remote_copy(
        src_ref=part.at[pl.ds(other_c * 2, 2)], dst_ref=r1_recv,
        send_sem=r_sems.at[0, 0], recv_sem=r_sems.at[1, 0],
        device_id=quad_peer(1), device_id_type=MESH,
    )
    r2_copy = pltpu.make_async_remote_copy(
        src_ref=r2_send, dst_ref=r2_recv,
        send_sem=r_sems.at[0, 1], recv_sem=r_sems.at[1, 1],
        device_id=quad_peer(2), device_id_type=MESH,
    )

    def r3_copy(dz):
        return pltpu.make_async_remote_copy(
            src_ref=r3_send.at[lax.rem(z + dz, 8)], dst_ref=r3_recv.at[z],
            send_sem=r_sems.at[2, dz], recv_sem=r_sems.at[3, dz],
            device_id=line_peer(dz), device_id_type=MESH,
        )

    def capall_copy(dz):
        return pltpu.make_async_remote_copy(
            src_ref=cap_all.at[0], dst_ref=cap_all.at[dz],
            send_sem=capall_sems.at[0, dz], recv_sem=capall_sems.at[1, dz],
            device_id=line_peer(dz), device_id_type=MESH,
        )

    def ring_right(k, h, s):
        src, dst = kv.at[h, s - 1, k], kv.at[h, s, k]
        if s == 4:
            src, dst = src.at[0], dst.at[0]
        return pltpu.make_async_remote_copy(
            src_ref=src, dst_ref=dst, send_sem=right_send.at[k, h, s - 1],
            recv_sem=right_recv.at[k, h, s - 1], device_id=line_peer(1), device_id_type=MESH,
        )

    def ring_left(k, h, s):
        src, dst = kv.at[h, (9 - s) % 8, k], kv.at[h, 8 - s, k]
        if s == 4:
            src, dst = src.at[1], dst.at[1]
        return pltpu.make_async_remote_copy(
            src_ref=src, dst_ref=dst, send_sem=left_send.at[k, h, s - 1],
            recv_sem=left_recv.at[k, h, s - 1], device_id=line_peer(7), device_id_type=MESH,
        )

    def query_copy(h, j):
        return pltpu.make_async_remote_copy(
            src_ref=q_buf.at[h, 2 if j == 3 else 0], dst_ref=q_buf.at[h, j],
            send_sem=q_send.at[h, j], recv_sem=q_recv.at[h, j],
            device_id=quad_peer(2 if j == 2 else 1), device_id_type=MESH,
        )

    def query_onward():
        def head(h, carry):
            query_copy(h, 2).wait_recv()
            query_copy(h, 3).start()
            return carry

        lax.fori_loop(0, HEADS_HERE, head, 0)

    def forward(k, h, s):
        ring_right(k, h, s - 1).wait_recv()
        ring_right(k, h, s).start()
        ring_left(k, h, s - 1).wait_recv()
        ring_left(k, h, s).start()

    def project(k):
        def head(h, carry):
            rows = tok[k].reshape(PART * 8, D)
            projected = jnp.dot(rows, w_qkv[h], preferred_element_type=F32)
            kv[h, 0, k, 0] = root_norm(projected[:, 128:256], gains_ref[1:2, :])
            kv[h, 0, k, 1] = projected[:, 256:384].astype(BF16)
            ring_right(k, h, 1).start()
            ring_left(k, h, 1).start()
            q_buf[h, 0, k] = root_norm(projected[:, 0:128], gains_ref[0:1, :] * QUERY_SCALE)
            if k == PARTS - 1:
                for j in (2, 1):
                    query_copy(h, j).start()
            return carry

        lax.fori_loop(0, HEADS_HERE, head, 0)

    def cap_columns():
        a1_recv[quad] = a1_send[quad]
        for j in range(1, 4):
            a1_copy(j).wait_recv()
        by_quad = a1_recv[...].astype(F32)
        for z_ in range(8):
            rows = jnp.concatenate([by_quad[i, 8 * z_ : 8 * z_ + 8] for i in range(4)], axis=0)
            a2_send[z_] = rows.astype(BF16)
        for dz in range(1, 8):
            a2_copy(dz).start()
        a2_recv[z] = a2_send[z]

    def cap_partial():
        load_cap.wait()
        for dz in range(1, 8):
            a2_copy(dz).wait_recv()
        cap_rows = a2_recv[...].reshape(256, 128)
        for h in range(HEADS_HERE):
            product = jnp.dot(cap_rows, w_cap[h], preferred_element_type=F32)
            both = jnp.concatenate(
                [product[:, :128].reshape(8, 4, 8, 128), product[:, 128:].reshape(8, 4, 8, 128)],
                axis=2,
            )
            for i in range(4):
                part[i, :, :, h * 128 : (h + 1) * 128] = both[:, i].astype(BF16)
        r1_copy.start()

    def cap_cores():
        r1_copy.wait_recv()
        r2_send[...] = (part[c * 2 + other_xl].astype(F32) + r1_recv[other_xl].astype(F32)).astype(BF16)
        r2_copy.start()

    def cap_x():
        r2_copy.wait_recv()
        r3_send[...] = (
            part[quad].astype(F32) + r1_recv[xl].astype(F32) + r2_recv[...].astype(F32)
        ).astype(BF16)
        for dz in range(1, 8):
            r3_copy(dz).start()
        r3_recv[z] = r3_send[z]

    def cap_line():
        for dz in range(1, 8):
            r3_copy(dz).wait_recv()
        total = jnp.sum(r3_recv[...].astype(F32), axis=0)
        for h in range(HEADS_HERE):
            cols = slice(h * 128, (h + 1) * 128)
            key_rows = root_norm(total[0:8, cols], gains_ref[2:3, :]).astype(F32)
            cap_all[0, :, cols] = jnp.concatenate([key_rows, total[8:16, cols]], axis=0).astype(BF16)
        for dz in range(1, 8):
            capall_copy(dz).start()

    def forward_all(k, s):
        def head(h, carry):
            forward(k, h, s)
            return carry

        lax.fori_loop(0, HEADS_HERE, head, 0)

    def attend(h, slots, first=False, caption=None):
        q = q_buf[h].reshape(QUERIES, HEAD)
        keys = [jnp.concatenate([kv[h, s, k, 0] for k in range(PARTS)], axis=0) for s in slots]
        values = [jnp.concatenate([kv[h, s, k, 1] for k in range(PARTS)], axis=0) for s in slots]
        if caption is not None:
            keys.append(caption[0])
            values.append(caption[1])
        scores = [
            lax.dot_general(q, k, (((1,), (1,)), ((), ())), preferred_element_type=F32)
            for k in keys
        ]
        halves = [s[:, i : i + 128] for s in scores for i in range(0, s.shape[1], 128)]
        top = halves[0]
        for s in halves[1 : 2 * len(slots)]:
            top = jnp.maximum(top, s)
        top = jnp.max(top, axis=-1, keepdims=True)
        for s in halves[2 * len(slots) :]:
            top = jnp.maximum(top, jnp.max(s, axis=-1, keepdims=True))
        if first:
            m_new = jnp.broadcast_to(top, (QUERIES, 128))
        else:
            m_old = m_buf[h]
            m_new = jnp.maximum(m_old, top)
        wide = jnp.concatenate([m_new, m_new], axis=1)
        update = None
        for s, v in zip(scores, values):
            weights = jnp.exp2(s - wide[:, : s.shape[1]]).astype(BF16)
            filled = jnp.concatenate([v, jnp.ones(v.shape, BF16)], axis=1)
            term = jnp.dot(weights, filled, preferred_element_type=F32)
            update = term if update is None else update + term
        if first:
            acc[h] = update
        else:
            alpha = jnp.exp2(m_old - m_new)
            acc[h] = acc[h] * jnp.concatenate([alpha, alpha], axis=1) + update
        m_buf[h] = m_new

    token_onward(0)
    cap_columns()
    cap_partial()
    token_rest(0)
    token_near(1)
    load_qkv.wait()
    cap_cores()
    project(0)
    token_onward(1)
    cap_x()
    forward_all(0, 2)
    token_rest(1)
    project(1)
    cap_line()
    forward_all(1, 2)
    query_onward()
    forward_all(0, 3)

    def step_three(h, carry):
        forward(1, h, 3)
        for j in (1, 3):
            query_copy(h, j).wait_recv()
        attend(h, [0, 1], first=True)
        attend(h, [7, 2])
        return carry

    lax.fori_loop(0, HEADS_HERE, step_three, 0)

    forward_all(0, 4)
    for dz in range(1, 8):
        capall_copy(dz).wait_recv()

    def step_four(h, carry):
        forward(1, h, 4)
        col = pl.ds(pl.multiple_of(h * 128, 128), 128)
        cap_kv = cap_all[:, :, col].astype(F32)
        cap_keys = cap_kv[:, 0:8, :].reshape(64, 128).astype(BF16)
        cap_values = cap_kv[:, 8:16, :].reshape(64, 128).astype(BF16)
        attend(h, [6, 3])
        attend(h, [5], caption=(cap_keys, cap_values))
        return carry

    lax.fori_loop(0, HEADS_HERE, step_four, 0)

    def core_copy(h):
        return pltpu.make_async_remote_copy(
            src_ref=o_send.at[h], dst_ref=o_recv.at[h],
            send_sem=o_ssem.at[h, 0], recv_sem=o_rsem.at[h, 0],
            device_id=quad_peer(1), device_id_type=MESH,
        )

    def core_level_copy(h):
        return pltpu.make_async_remote_copy(
            src_ref=l_send.at[h], dst_ref=l_recv.at[h],
            send_sem=o_ssem.at[h, 1], recv_sem=o_rsem.at[h, 1],
            device_id=quad_peer(1), device_id_type=MESH,
        )

    def x_copy(h):
        return pltpu.make_async_remote_copy(
            src_ref=ox_send.at[h], dst_ref=ox_recv.at[h],
            send_sem=o_ssem.at[h, 2], recv_sem=o_rsem.at[h, 2],
            device_id=quad_peer(2), device_id_type=MESH,
        )

    def x_level_copy(h):
        return pltpu.make_async_remote_copy(
            src_ref=lx_send.at[h], dst_ref=lx_recv.at[h],
            send_sem=o_ssem.at[h, 3], recv_sem=o_rsem.at[h, 3],
            device_id=quad_peer(2), device_id_type=MESH,
        )

    def partial_output(h, j):
        rows = slice(j * BLOCK, (j + 1) * BLOCK)
        denominator = acc[h, rows, 128:]
        return acc[h, rows, :128] / denominator, m_buf[h, rows, :] + jnp.log(denominator) * LOG2E

    def wide_level(level):
        return jnp.broadcast_to(level[0:1, :], (128, BLOCK)).T

    def merge(terms):
        top = terms[0][1]
        for _, level in terms[1:]:
            top = jnp.maximum(top, level)
        numerator, weight = None, None
        for out, level in terms:
            share = jnp.exp2(level - top)
            numerator = out * share if numerator is None else numerator + out * share
            weight = share if weight is None else weight + share
        return (numerator / weight).astype(BF16), top, weight

    def step_last(h):
        for k in range(PARTS):
            ring_right(k, h, 4).wait_recv()
            ring_left(k, h, 4).wait_recv()
        attend(h, [4])
        for i, j in enumerate((1, 3)):
            out, level = partial_output(h, j)
            o_send[h, i] = out.astype(BF16)
            l_send[h, i] = level.T[0:8, :]
        core_copy(h).start()
        core_level_copy(h).start()

    def step_pair(h):
        core_copy(h).wait_recv()
        core_level_copy(h).wait_recv()
        out, top, weight = merge(
            [partial_output(h, 2), (o_recv[h, 1].astype(F32), wide_level(l_recv[h, 1]))]
        )
        ox_send[h] = out
        lx_send[h] = (top + jnp.log(weight) * LOG2E).T[0:8, :]
        x_copy(h).start()
        x_level_copy(h).start()

    def last_loop(h, carry):
        step_last(h)
        return carry

    lax.fori_loop(0, HEADS_HERE, last_loop, 0)

    def pair_loop(h, carry):
        step_pair(h)
        return carry

    lax.fori_loop(0, HEADS_HERE, pair_loop, 0)

    def combine(h, carry):
        x_copy(h).wait_recv()
        x_level_copy(h).wait_recv()
        att[h] = merge(
            [
                partial_output(h, 0),
                (o_recv[h, 0].astype(F32), wide_level(l_recv[h, 0])),
                (ox_recv[h].astype(F32), wide_level(lx_recv[h])),
            ]
        )[0]
        return carry

    lax.fori_loop(0, HEADS_HERE, combine, 0)

    load_out.wait()

    def p_copy(n, i):
        source, (dy, dx) = REDUCE_HOPS[i]
        return pltpu.make_async_remote_copy(
            src_ref=p_send.at[n, source], dst_ref=p_recv.at[n, i],
            send_sem=p_ssem.at[n, i], recv_sem=p_rsem.at[n, i],
            device_id={"ulysses": ulysses_peer(dy, dx)}, device_id_type=MESH,
        )

    def out_chunk(n, carry):
        cols = pl.ds(pl.multiple_of(n * CHUNK, 128), CHUNK)
        rows = jnp.concatenate([att[h] for h in range(HEADS_HERE)], axis=1)
        product = jnp.dot(rows, w_out[:, cols], preferred_element_type=F32)
        product = product.reshape(PARTS, 8, PART, CHUNK)
        for i in (5, 6, 7, 3):
            p_send[n, i] = product[:, i].reshape(ROWS, CHUNK).astype(BF16)
        for i in range(4):
            p_copy(n, i).start()
        for k, i in enumerate((0, 1, 2, 4)):
            p_keep[n, k] = product[:, i].reshape(ROWS, CHUNK)
        return carry

    lax.fori_loop(0, CHUNKS, out_chunk, 0)

    def pass_on(n, carry):
        for k, i in ((1, 0), (2, 1), (3, 2)):
            p_copy(n, i).wait_recv()
            source = REDUCE_HOPS[i + 4][0]
            p_send[n, source] = (p_keep[n, k] + p_recv[n, i].astype(F32)).astype(BF16)
            p_copy(n, i + 4).start()
        return carry

    lax.fori_loop(0, CHUNKS, pass_on, 0)

    def finish(n, carry):
        cols = pl.ds(pl.multiple_of(n * CHUNK, 128), CHUNK)
        for i in range(3, 7):
            p_copy(n, i).wait_recv()
        projection = p_keep[n, 0] + jnp.sum(p_recv[n, 3:7].astype(F32), axis=0)
        out_ref[:, cols] = (
            img_ref[:, cols].astype(F32) + mod_ref[2:3, cols] * projection
        ).astype(BF16)
        return carry

    lax.fori_loop(0, CHUNKS, finish, 0)

    for j in range(1, 4):
        a1_copy(j).wait_send()
    r1_copy.wait_send()
    r2_copy.wait_send()
    for dz in range(1, 8):
        a2_copy(dz).wait_send()
        r3_copy(dz).wait_send()
        capall_copy(dz).wait_send()
    for k in range(PARTS):
        for i in range(7):
            token_copy(k, i).wait_send()

    def drain_head(h, carry):
        for s in range(1, 5):
            for k in range(PARTS):
                ring_right(k, h, s).wait_send()
                ring_left(k, h, s).wait_send()
        for j in range(1, 4):
            query_copy(h, j).wait_send()
        core_copy(h).wait_send()
        core_level_copy(h).wait_send()
        x_copy(h).wait_send()
        x_level_copy(h).wait_send()
        return carry

    lax.fori_loop(0, HEADS_HERE, drain_head, 0)

    def drain_chunk(n, carry):
        for i in range(7):
            p_copy(n, i).wait_send()
        return carry

    lax.fori_loop(0, CHUNKS, drain_chunk, 0)


def per_device(
    image_tokens, text_tokens, modulation, text_modulation, norm_gains,
    qkv_weight, text_kv_weight, out_weight,
):
    qkv = jnp.transpose(qkv_weight, (1, 0, 2))
    tkv = jnp.transpose(text_kv_weight, (1, 0, 2))
    dma = pltpu.SemaphoreType.DMA
    vmem = pl.BlockSpec(memory_space=pltpu.VMEM)
    hbm = pl.BlockSpec(memory_space=pl.ANY)
    h3 = HEADS_HERE
    return pl.pallas_call(
        kernel,
        out_shape=jax.ShapeDtypeStruct((ROWS, D), BF16),
        in_specs=[hbm] * 8,
        out_specs=vmem,
        scratch_shapes=[
            pltpu.VMEM((ROWS, D), BF16),
            pltpu.VMEM((CAP_ROWS, D), BF16),
            pltpu.VMEM((3, D), F32),
            pltpu.VMEM((2, D), F32),
            pltpu.VMEM((3, HEAD), F32),
            pltpu.VMEM((h3, D, 384), BF16),
            pltpu.VMEM((h3, 128, 256), BF16),
            pltpu.VMEM((384, D), BF16),
            pltpu.VMEM((PARTS, 8, PART, D), BF16),
            pltpu.VMEM((4, 64, 128), BF16),
            pltpu.VMEM((4, 64, 128), BF16),
            pltpu.VMEM((8, 32, 128), BF16),
            pltpu.VMEM((8, 32, 128), BF16),
            pltpu.VMEM((4, 8, 16, 384), BF16),
            pltpu.VMEM((2, 8, 16, 384), BF16),
            pltpu.VMEM((8, 16, 384), BF16),
            pltpu.VMEM((8, 16, 384), BF16),
            pltpu.VMEM((8, 16, 384), BF16),
            pltpu.VMEM((8, 16, 384), BF16),
            pltpu.VMEM((8, 16, 384), BF16),
            pltpu.VMEM((h3, 4, PARTS, BLOCK // PARTS, 128), BF16),
            pltpu.VMEM((h3, 8, PARTS, 2, BLOCK // PARTS, 128), BF16),
            pltpu.VMEM((h3, QUERIES, 128), F32),
            pltpu.VMEM((h3, QUERIES, 256), F32),
            pltpu.VMEM((h3, 2, BLOCK, 128), BF16),
            pltpu.VMEM((h3, 2, BLOCK, 128), BF16),
            pltpu.VMEM((h3, 2, 8, BLOCK), F32),
            pltpu.VMEM((h3, 2, 8, BLOCK), F32),
            pltpu.VMEM((h3, BLOCK, 128), BF16),
            pltpu.VMEM((h3, BLOCK, 128), BF16),
            pltpu.VMEM((h3, 8, BLOCK), F32),
            pltpu.VMEM((h3, 8, BLOCK), F32),
            pltpu.VMEM((h3, BLOCK, 128), BF16),
            pltpu.VMEM((CHUNKS, 8, ROWS, CHUNK), BF16),
            pltpu.VMEM((CHUNKS, 7, ROWS, CHUNK), BF16),
            pltpu.VMEM((CHUNKS, 4, ROWS, CHUNK), F32),
            dma((8,)), dma((PARTS, 7)), dma((PARTS, 7)), dma((4, 8)), dma((4, 8)), dma((2, 8)),
            dma((h3, 4)), dma((h3, 4)),
            dma((PARTS, h3, 4)), dma((PARTS, h3, 4)), dma((PARTS, h3, 4)), dma((PARTS, h3, 4)),
            dma((h3, 4)), dma((h3, 4)),
            dma((CHUNKS, 7)), dma((CHUNKS, 7)),
        ],
        compiler_params=pltpu.CompilerParams(
            collective_id=0, has_side_effects=True, vmem_limit_bytes=60 * 1024 * 1024
        ),
        name="joint_attention",
    )(image_tokens, text_tokens, modulation, text_modulation, norm_gains, qkv, tkv, out_weight)


def solution(mesh):
    in_specs = (
        P(("blk", "ulysses"), None),
        P("blk", None),
        P(),
        P(),
        P(),
        P(None, "ulysses", None),
        P("blk", "ulysses", None),
        P("ulysses", None),
    )
    out_specs = P(("blk", "ulysses"), None)
    return jax.shard_map(
        per_device, mesh=mesh, in_specs=in_specs, out_specs=out_specs, check_vma=False
    )
```
